32 devices in a mesh: dp: 8 (over z, x), group: 4 (over y, core).
Axes of the slice: x: 2, y: 2, z: 4, core: 2. Of those that a mesh axis runs over, the one named last changes fastest.
Arguments:
- hidden_in: bfloat16 [16, 256, 576], P('dp', 'group'), may hold values from -4 to 4
- out_grad: bfloat16 [16, 256, 576], P('dp', 'group'), may hold values from -6 to 6
- span_order: int32 [16, 8], P('dp'), may hold values from 0 to 7, each once within a row
- weights: float32 [3538944], P('group'), may hold values from -2 to 2
- first_moment: float32 [3538944], P('group'), may hold values from -30 to 30
- second_moment: float32 [3538944], P('group'), may hold values from 10 to 1000
- gains: float32 [2, 576], P(None, 'group'), may hold values from 0.5 to 1.5
- gain_first: float32 [2, 576], P(None, 'group'), may hold values from -30 to 30
- gain_second: float32 [2, 576], P(None, 'group'), may hold values from 10 to 1000
Outputs:
- block_out: float32 [16, 256, 576], P('dp', 'group')
- in_grad: float32 [16, 256, 576], P('dp', 'group')
- weight_grad: float32 [3538944], P('group')
- gain_grad: float32 [2, 576], P(None, 'group')
- new_weights: float32 [3538944], P('group')
- new_first: float32 [3538944], P('group')
- new_second: float32 [3538944], P('group')
- new_gains: float32 [2, 576], P(None, 'group')
- new_gain_first: float32 [2, 576], P(None, 'group')
- new_gain_second: float32 [2, 576], P(None, 'group')
The draws below stay inside these ranges and needn't reach their ends.
Inputs may be any that keep to these rules, and one draw needn't show every extreme that they name: Each row of span_order is a permutation of the 8 blocks of positions of its sequence.
All inputs are finite; a program needn't handle non-finite values.
Results may differ from the reference program's by a relative error of at most 0.014.
The reference program's roundings to bfloat16 on the way count: a program that leaves them out, or rounds other values in their place, can miss the bound.
Values may be sent and summed in bfloat16 or wider, within the bound.
A program may use at most 128 MiB of HBM per device.

```python
import math
import jax
import jax.numpy as jnp
from jax import lax

D = 576
HEADS = 9
KV_HEADS = 3
HEAD_DIM = 64
FF = 1536
SPAN = 32
SEQ_DEV = 2
NCHUNK = 8
SEQ_LEN = 256
SEQS = 16
PARAMS = 3538944
N_DP = 8
N_GROUP = 4


def draw_hidden_in(key, part):
    full_shape = (SEQS, SEQ_LEN, D)
    return jnp.clip(jax.random.normal(jax.random.fold_in(key, 1), full_shape, jnp.float32), -4.0, 4.0).astype(jnp.bfloat16)


def draw_weights(key, part):
    q_width = HEADS * HEAD_DIM
    kv_width = KV_HEADS * HEAD_DIM
    layout = [(D, q_width, D), (D, kv_width, D), (D, kv_width, D), (q_width, D, q_width / 9.0), (D, FF, D), (D, FF, D), (FF, D, FF)]
    pieces = []
    for index_num, layer_entry in enumerate(layout):
        sub_key = jax.random.fold_in(key, 10 + index_num)
        dims_pair = (layer_entry[0], layer_entry[1])
        unit_draw = jnp.clip(jax.random.normal(sub_key, dims_pair, jnp.float32), -4.0, 4.0)
        pieces.append(unit_draw / math.sqrt(layer_entry[2]))
    return jnp.concatenate([block_piece.reshape(-1) for block_piece in pieces])


def block_scale(rng, extent, shards, smallest, largest):
    def one(dim, blocks):
        heights = jax.random.uniform(jax.random.fold_in(jax.random.fold_in(rng, 6), dim), (blocks,), jnp.float32, smallest / len(shards), largest / len(shards))
        return jnp.repeat(jnp.exp(heights), extent[dim] // blocks).reshape((-1,) + (1,) * (len(extent) - dim - 1))

    loudness = one(*shards[0])
    for cut in shards[1:]:
        loudness = loudness * one(*cut)
    return loudness


def centred(rng, shape, scale, most, cuts=(), held_as=jnp.bfloat16):
    entries = jax.random.normal(rng, shape, jnp.float32) * scale
    if len(cuts) > 0:
        entries = block_scale(rng, shape, cuts, -0.22, 0.18) * entries
    return jnp.clip(entries, min=-most, max=most).astype(held_as)


def setup_inputs(seed: int = 0) -> dict:
    streams_of = jax.random.split(jax.random.key(seed), 10)
    hidden_in = draw_hidden_in(jax.random.fold_in(streams_of[9], 71), 0)
    out_grad = centred(streams_of[1], (SEQS, SEQ_LEN, D), 1.0, 6.0, ((0, 8), (1, 4)))
    span_order = jax.vmap(lambda own: jax.random.permutation(own, NCHUNK))(jax.random.split(streams_of[2], SEQS)).reshape((SEQS, NCHUNK)).astype(jnp.int32)
    weights = draw_weights(jax.random.fold_in(streams_of[9], 71), 0)
    first_moment = centred(streams_of[4], (PARAMS,), 5.0, 30.0, ((0, 4),), jnp.float32)
    second_moment = jnp.clip(jnp.exp(math.log(1000.0) - 4.6051702 * jax.random.uniform(streams_of[5], (PARAMS,), jnp.float32) ** block_scale(streams_of[5], (PARAMS,), ((0, 4),), -0.2, 0.2)), 10.0, 1000.0)
    gains = jnp.clip(1.0 + 0.1 * jax.random.normal(streams_of[6], (2, D), jnp.float32), 0.5, 1.5)
    gain_first = centred(streams_of[7], (2, D), 5.0, 30.0, ((1, 4),), jnp.float32)
    gain_second = jnp.clip(jnp.exp(math.log(1000.0) - 4.6051702 * jax.random.uniform(streams_of[8], (2, D), jnp.float32) ** block_scale(streams_of[8], (2, D), ((1, 4),), -0.2, 0.2)), 10.0, 1000.0)
    return {"hidden_in": hidden_in, "out_grad": out_grad, "span_order": span_order, "weights": weights, "first_moment": first_moment, "second_moment": second_moment, "gains": gains, "gain_first": gain_first, "gain_second": gain_second}


EPS_NORM = 1e-05
ROPE_BASE = 100000.0
BETA_ONE = 0.9
BETA_TWO = 0.95
LEARN_RATE = 0.02
GAIN_RATE = 0.25
DECAY_RATE = 0.1
EPS_ADAM = 1e-08
CORRECT_ONE = 1.0 - 0.9 ** 5
CORRECT_TWO = 1.0 - 0.95 ** 5
NEG_LARGE = -1e+30

def split_weights(flat_vector):
    q_width = HEADS * HEAD_DIM
    kv_width = KV_HEADS * HEAD_DIM
    layout = [(D, q_width), (D, kv_width), (D, kv_width), (q_width, D), (D, FF), (D, FF), (FF, D)]
    pieces = []
    offset = 0
    for rows_cols in layout:
        amount = rows_cols[0] * rows_cols[1]
        pieces.append(lax.slice_in_dim(flat_vector, offset, offset + amount, axis=0).reshape(rows_cols))
        offset = offset + amount
    return pieces

def rope_tables(positions):
    freq_index = jnp.arange(HEAD_DIM // 2, dtype=jnp.float32)
    inverse = ROPE_BASE ** (-2.0 * freq_index / HEAD_DIM)
    angles = positions.astype(jnp.float32)[:, None] * inverse[None, :]
    return (jnp.cos(angles), jnp.sin(angles))

def rotate(vectors, cosine, sine_table):
    half_dim = HEAD_DIM // 2
    first_half = vectors[..., :half_dim]
    second_half = vectors[..., half_dim:]
    cos_b = cosine[:, None, :]
    sin_b = sine_table[:, None, :]
    return jnp.concatenate([first_half * cos_b - second_half * sin_b, second_half * cos_b + first_half * sin_b], axis=-1)

def rotate_back(vectors, cosine, sine_table):
    half_dim = HEAD_DIM // 2
    first_half = vectors[..., :half_dim]
    second_half = vectors[..., half_dim:]
    cos_b = cosine[:, None, :]
    sin_b = sine_table[:, None, :]
    return jnp.concatenate([first_half * cos_b + second_half * sin_b, second_half * cos_b - first_half * sin_b], axis=-1)

def norm_forward(vectors):
    factor = lax.rsqrt(lax.optimization_barrier(jnp.mean(vectors * vectors, axis=-1, keepdims=True)) + EPS_NORM)
    return (vectors * factor, factor)

def norm_backward(grad_normed, normed, factor):
    return factor * (grad_normed - normed * lax.optimization_barrier(jnp.mean(grad_normed * normed, axis=-1, keepdims=True)))

def group_outer(left_rows, right_rows):
    left_f = left_rows.astype(jnp.float32).reshape(N_GROUP, -1, left_rows.shape[-1])
    right_f = right_rows.astype(jnp.float32).reshape(N_GROUP, -1, right_rows.shape[-1])
    return jnp.einsum('gti,gtj->gij', left_f, right_f)

def adamw_step(param_now, moment_one, moment_two, grad_now, decay_weight, step_rate):
    first_new = BETA_ONE * moment_one + (1.0 - BETA_ONE) * grad_now
    second_new = BETA_TWO * moment_two + (1.0 - BETA_TWO) * grad_now * grad_now
    update = first_new / CORRECT_ONE / (jnp.sqrt(second_new / CORRECT_TWO) + EPS_ADAM)
    return (param_now - step_rate * (update + decay_weight * param_now), first_new, second_new)

def sequence_pass(tokens, cotangent, order_row, matrices, gain_attn, gain_ffn):
    w_query, w_key, w_value, w_out, w_gate, w_up, w_down = matrices
    group_size = HEADS // KV_HEADS
    scale = HEAD_DIM ** (-0.5)
    positions = (order_row[:, None] * SPAN + jnp.arange(SPAN, dtype=jnp.int32)[None, :]).reshape(-1)
    cosine, sine_table = rope_tables(positions)
    residual = tokens.astype(jnp.float32)
    normed_one, factor_one = norm_forward(residual)
    attn_in = (normed_one * gain_attn).astype(jnp.bfloat16)
    query_proj = jnp.dot(attn_in, w_query, preferred_element_type=jnp.float32).reshape(-1, HEADS, HEAD_DIM)
    key_proj = jnp.dot(attn_in, w_key, preferred_element_type=jnp.float32).reshape(-1, KV_HEADS, HEAD_DIM)
    value_proj = jnp.dot(attn_in, w_value, preferred_element_type=jnp.float32)
    query_b = rotate(query_proj, cosine, sine_table).astype(jnp.bfloat16)
    key_b = rotate(key_proj, cosine, sine_table).astype(jnp.bfloat16)
    value_b = value_proj.astype(jnp.bfloat16)
    query_f = query_b.astype(jnp.float32).reshape(-1, KV_HEADS, group_size, HEAD_DIM)
    key_f = key_b.astype(jnp.float32)
    value_f = value_b.astype(jnp.float32).reshape(-1, KV_HEADS, HEAD_DIM)
    scores = jnp.einsum('qkgd,skd->kgqs', query_f, key_f) * scale
    allowed = positions[None, :] <= positions[:, None]
    scores = jnp.where(allowed[None, None], scores, NEG_LARGE)
    row_max = lax.optimization_barrier(jnp.max(scores, axis=-1))
    log_total = row_max + jnp.log(lax.optimization_barrier(jnp.sum(jnp.exp(scores - row_max[..., None]), axis=-1)))
    probs = jnp.exp(scores - log_total[..., None])
    probs_b = probs.astype(jnp.bfloat16)
    probs_f = probs_b.astype(jnp.float32)
    attn_vals = jnp.einsum('kgqs,skd->qkgd', probs_f, value_f)
    attn_b = attn_vals.reshape(attn_vals.shape[0], -1).astype(jnp.bfloat16)
    middle = residual + jnp.dot(attn_b, w_out, preferred_element_type=jnp.float32)
    normed_two, factor_two = norm_forward(middle)
    ffn_in = (normed_two * gain_ffn).astype(jnp.bfloat16)
    gate_proj = jnp.dot(ffn_in, w_gate, preferred_element_type=jnp.float32)
    up_proj = jnp.dot(ffn_in, w_up, preferred_element_type=jnp.float32)
    sigmoid_gate = jax.nn.sigmoid(gate_proj)
    hidden = (gate_proj * sigmoid_gate * up_proj).astype(jnp.bfloat16)
    block_out = middle + jnp.dot(hidden, w_down, preferred_element_type=jnp.float32)
    grad_hidden = jnp.dot(cotangent, w_down.T, preferred_element_type=jnp.float32)
    grad_gate = (grad_hidden * up_proj * sigmoid_gate * (1.0 + gate_proj * (1.0 - sigmoid_gate))).astype(jnp.bfloat16)
    grad_up = (grad_hidden * gate_proj * sigmoid_gate).astype(jnp.bfloat16)
    grad_ffn_in = jnp.dot(grad_gate, w_gate.T, preferred_element_type=jnp.float32) + jnp.dot(grad_up, w_up.T, preferred_element_type=jnp.float32)
    grad_middle = cotangent.astype(jnp.float32) + norm_backward(grad_ffn_in * gain_ffn, normed_two, factor_two)
    grad_middle_b = grad_middle.astype(jnp.bfloat16)
    grad_attn = jnp.dot(grad_middle_b, w_out.T, preferred_element_type=jnp.float32).astype(jnp.bfloat16)
    grad_attn_f = grad_attn.astype(jnp.float32).reshape(-1, KV_HEADS, group_size, HEAD_DIM)
    attn_f = attn_b.astype(jnp.float32).reshape(-1, KV_HEADS, group_size, HEAD_DIM)
    delta_rows = jnp.einsum('qkgd,qkgd->kgq', grad_attn_f, attn_f)
    grad_probs = jnp.einsum('qkgd,skd->kgqs', grad_attn_f, value_f)
    grad_scores = (probs * (grad_probs - delta_rows[..., None]) * scale).astype(jnp.bfloat16).astype(jnp.float32)
    grad_query = jnp.einsum('kgqs,skd->qkgd', grad_scores, key_f).reshape(-1, HEADS, HEAD_DIM)
    grad_key = jnp.einsum('kgqs,qkgd->skd', grad_scores, query_f)
    grad_value = jnp.einsum('kgqs,qkgd->skd', probs_f, grad_attn_f)
    grad_query_b = rotate_back(grad_query, cosine, sine_table).reshape(-1, HEADS * HEAD_DIM).astype(jnp.bfloat16)
    grad_key_b = rotate_back(grad_key, cosine, sine_table).reshape(-1, KV_HEADS * HEAD_DIM).astype(jnp.bfloat16)
    grad_value_b = grad_value.reshape(-1, KV_HEADS * HEAD_DIM).astype(jnp.bfloat16)
    grad_attn_in = jnp.dot(grad_query_b, w_query.T, preferred_element_type=jnp.float32)
    grad_attn_in = grad_attn_in + jnp.dot(grad_key_b, w_key.T, preferred_element_type=jnp.float32)
    grad_attn_in = grad_attn_in + jnp.dot(grad_value_b, w_value.T, preferred_element_type=jnp.float32)
    in_grad = grad_middle + norm_backward(grad_attn_in * gain_attn, normed_one, factor_one)
    grads = (group_outer(attn_in, grad_query_b), group_outer(attn_in, grad_key_b), group_outer(attn_in, grad_value_b), group_outer(attn_b, grad_middle_b), group_outer(ffn_in, grad_gate), group_outer(ffn_in, grad_up), group_outer(hidden, cotangent))
    gg_attn = lax.optimization_barrier(jnp.sum((grad_attn_in * normed_one).reshape(N_GROUP, -1, D), axis=1))
    gg_ffn = lax.optimization_barrier(jnp.sum((grad_ffn_in * normed_two).reshape(N_GROUP, -1, D), axis=1))
    return (block_out, in_grad, grads, jnp.stack([gg_attn, gg_ffn], axis=1))

def round_sum(partial_item):
    return lax.optimization_barrier(jnp.sum(lax.optimization_barrier(partial_item.astype(jnp.bfloat16)).astype(jnp.float32), axis=0))

def reference(hidden_in, out_grad, span_order, weights, first_moment, second_moment, gains, gain_first, gain_second):
    matrices = split_weights(weights.astype(jnp.bfloat16))
    gain_round = lax.optimization_barrier(gains.astype(jnp.bfloat16)).astype(jnp.float32)
    gain_attn = gain_round[0]
    gain_ffn = gain_round[1]
    blocks_in = hidden_in.reshape(N_DP, SEQ_DEV, SEQ_LEN, D)
    blocks_grad = out_grad.reshape(N_DP, SEQ_DEV, SEQ_LEN, D)
    blocks_order = span_order.reshape(N_DP, SEQ_DEV, NCHUNK)

    def per_block(totals, block_inputs):

        def per_sequence(carried, inputs):
            tokens, cotangent, order_row = inputs
            block_out, in_grad, grads, gain_terms = sequence_pass(tokens, cotangent, order_row, matrices, gain_attn, gain_ffn)
            weight_parts, gain_parts = carried
            weight_parts = tuple((total + grad_item for total, grad_item in zip(weight_parts, grads)))
            return ((weight_parts, gain_parts + gain_terms), (block_out, in_grad))
        start_parts = tuple((jnp.zeros((N_GROUP,) + matrix.shape, jnp.float32) for matrix in matrices))
        start_gains = jnp.zeros((N_GROUP, 2, D), jnp.float32)
        (weight_parts, gain_parts), outputs = lax.scan(per_sequence, (start_parts, start_gains), block_inputs)
        weight_totals, gain_totals = totals
        weight_totals = tuple((total + round_sum(part_item) for total, part_item in zip(weight_totals, weight_parts)))
        return ((weight_totals, gain_totals + round_sum(gain_parts)), outputs)
    start_totals = tuple((jnp.zeros(matrix.shape, jnp.float32) for matrix in matrices))
    (weight_sums, gain_grad), (block_out, in_grad) = lax.scan(per_block, (start_totals, jnp.zeros((2, D), jnp.float32)), (blocks_in, blocks_grad, blocks_order))
    block_out = block_out.reshape(SEQS, SEQ_LEN, D)
    in_grad = in_grad.reshape(SEQS, SEQ_LEN, D)
    weight_grad = jnp.concatenate([grad_item.reshape(-1) for grad_item in weight_sums])
    new_weights, new_first, new_second = adamw_step(weights, first_moment, second_moment, weight_grad, DECAY_RATE, LEARN_RATE)
    new_gains, new_gain_first, new_gain_second = adamw_step(gains, gain_first, gain_second, gain_grad, 0.0, GAIN_RATE)
    return (block_out, in_grad, weight_grad, gain_grad, new_weights, new_first, new_second, new_gains, new_gain_first, new_gain_second)
```

```python
import functools

import jax
import jax.numpy as jnp
from jax import lax
from jax.experimental import pallas as pl
from jax.experimental.pallas import tpu as pltpu
from jax.sharding import PartitionSpec as P

D = 576
HEADS = 9
KV_HEADS = 3
HEAD_DIM = 64
FF = 1536
SPAN = 32


EPS_NORM = 1e-05
ROPE_BASE = 100000.0
BETA_ONE = 0.9
BETA_TWO = 0.95
LEARN_RATE = 0.02
GAIN_RATE = 0.25
DECAY_RATE = 0.1
EPS_ADAM = 1e-08
CORRECT_ONE = 1.0 - 0.9**5
CORRECT_TWO = 1.0 - 0.95**5
NEG_LARGE = -1e30


def split_weights(flat_vector):
    q_width = HEADS * HEAD_DIM
    kv_width = KV_HEADS * HEAD_DIM
    layout = [(D, q_width), (D, kv_width), (D, kv_width), (q_width, D), (D, FF), (D, FF), (FF, D)]
    pieces = []
    offset = 0
    for rows_cols in layout:
        amount = rows_cols[0] * rows_cols[1]
        pieces.append(
            lax.slice_in_dim(flat_vector, offset, offset + amount, axis=0).reshape(rows_cols)
        )
        offset = offset + amount
    return pieces


def rope_tables(positions):
    freq_index = jnp.arange(HEAD_DIM // 2, dtype=jnp.float32)
    inverse = ROPE_BASE ** (-2.0 * freq_index / HEAD_DIM)
    angles = positions.astype(jnp.float32)[:, None] * inverse[None, :]
    return (jnp.cos(angles), jnp.sin(angles))


def rotate(vectors, cosine, sine_table):
    half_dim = HEAD_DIM // 2
    first_half = vectors[..., :half_dim]
    second_half = vectors[..., half_dim:]
    cos_b = cosine[:, None, :]
    sin_b = sine_table[:, None, :]
    return jnp.concatenate(
        [first_half * cos_b - second_half * sin_b, second_half * cos_b + first_half * sin_b],
        axis=-1,
    )


def rotate_back(vectors, cosine, sine_table):
    half_dim = HEAD_DIM // 2
    first_half = vectors[..., :half_dim]
    second_half = vectors[..., half_dim:]
    cos_b = cosine[:, None, :]
    sin_b = sine_table[:, None, :]
    return jnp.concatenate(
        [first_half * cos_b + second_half * sin_b, second_half * cos_b - first_half * sin_b],
        axis=-1,
    )


def norm_forward(vectors):
    factor = lax.rsqrt(jnp.mean(vectors * vectors, axis=-1, keepdims=True) + EPS_NORM)
    return (vectors * factor, factor)


def norm_backward(grad_normed, normed, factor):
    return factor * (grad_normed - normed * jnp.mean(grad_normed * normed, axis=-1, keepdims=True))


def outer_sum(left_rows, right_rows):
    return lax.dot_general(
        left_rows, right_rows, (((0,), (0,)), ((), ())), preferred_element_type=jnp.float32
    )


def adamw_step(param_now, moment_one, moment_two, grad_now, decay_weight, step_rate):
    first_new = BETA_ONE * moment_one + (1.0 - BETA_ONE) * grad_now
    second_new = BETA_TWO * moment_two + (1.0 - BETA_TWO) * grad_now * grad_now
    update = first_new / CORRECT_ONE / (jnp.sqrt(second_new / CORRECT_TWO) + EPS_ADAM)
    return (param_now - step_rate * (update + decay_weight * param_now), first_new, second_new)


def split_pair(kv_seq):
    kv_width = KV_HEADS * HEAD_DIM
    key_blk = kv_seq[:, :kv_width].reshape(-1, KV_HEADS, HEAD_DIM)
    value_blk = kv_seq[:, kv_width:].reshape(-1, KV_HEADS, HEAD_DIM)
    return (key_blk, value_blk)


def masked_scores(query_blk, key_blk, query_pos, key_pos):
    scores = jnp.einsum(
        "qkgd,skd->kgqs", query_blk, key_blk, preferred_element_type=jnp.float32
    ) * HEAD_DIM ** (-0.5)
    allowed = key_pos[None, :] <= query_pos[:, None]
    return jnp.where(allowed[None, None], scores, NEG_LARGE)


def attend(query_blk, kv_seq, query_pos, key_pos):
    key_blk, value_blk = split_pair(kv_seq)
    scores = masked_scores(query_blk, key_blk, query_pos, key_pos)
    row_max = jnp.max(scores, axis=-1)
    log_total = row_max + jnp.log(jnp.sum(jnp.exp(scores - row_max[..., None]), axis=-1))
    probs_b = jnp.exp(scores - log_total[..., None]).astype(jnp.bfloat16)
    attn_vals = jnp.einsum("kgqs,skd->qkgd", probs_b, value_blk, preferred_element_type=jnp.float32)
    return (attn_vals.reshape(attn_vals.shape[0], -1).astype(jnp.bfloat16), log_total)


def attend_back(query_blk, kv_seq, query_pos, key_pos, log_total, attn_rows, grad_rows):
    group_size = HEADS // KV_HEADS
    key_blk, value_blk = split_pair(kv_seq)
    scores = masked_scores(query_blk, key_blk, query_pos, key_pos)
    probs = jnp.exp(scores - log_total[..., None])
    probs_b = probs.astype(jnp.bfloat16)
    grad_heads = grad_rows.reshape(-1, KV_HEADS, group_size, HEAD_DIM)
    attn_heads = attn_rows.reshape(-1, KV_HEADS, group_size, HEAD_DIM)
    delta_rows = jnp.einsum(
        "qkgd,qkgd->kgq", grad_heads, attn_heads, preferred_element_type=jnp.float32
    )
    grad_probs = jnp.einsum(
        "qkgd,skd->kgqs", grad_heads, value_blk, preferred_element_type=jnp.float32
    )
    grad_scores = (probs * (grad_probs - delta_rows[..., None]) * HEAD_DIM ** (-0.5)).astype(
        jnp.bfloat16
    )
    grad_query = jnp.einsum(
        "kgqs,skd->qkgd", grad_scores, key_blk, preferred_element_type=jnp.float32
    )
    grad_key = jnp.einsum(
        "kgqs,qkgd->skd", grad_scores, query_blk, preferred_element_type=jnp.float32
    )
    grad_value = jnp.einsum(
        "kgqs,qkgd->skd", probs_b, grad_heads, preferred_element_type=jnp.float32
    )
    key_rows = grad_key.shape[0]
    stacked = jnp.concatenate(
        [grad_key.reshape(key_rows, -1), grad_value.reshape(key_rows, -1)], axis=-1
    )
    return (grad_query, stacked)


LANES = 128
TILE = 16


def cut_evenly(total_units, most):
    count = max(1, min(most, total_units))
    base, extra = divmod(total_units, count)
    return [base + (1 if i < extra else 0) for i in range(count)]


def block_of(rows):
    for block in (144, 128, 96, 64, 48, 32):
        if rows % block == 0:
            return block
    return TILE


def over_rows(rows, step):
    block = block_of(rows)
    if rows == block:
        step(0, block)
        return

    def one(i, carry):
        step(pl.multiple_of(i * block, TILE), block)
        return carry

    lax.fori_loop(0, rows // block, one, 0)


def rows_at(start, size):
    return pl.ds(start if isinstance(start, int) else pl.multiple_of(start, TILE), size)


class Copies:
    def __init__(self, send_sem, recv_sem):
        self.send_sem, self.recv_sem, self.made = send_sem, recv_sem, []

    def start(self, src, dst, slot, where):
        copy = pltpu.make_async_remote_copy(
            src_ref=src,
            dst_ref=dst,
            send_sem=self.send_sem.at[slot],
            recv_sem=self.recv_sem.at[slot],
            device_id=where,
            device_id_type=pl.DeviceIdType.MESH,
        )
        copy.start()
        self.made.append(copy)

    def arrived(self, dst, slot, where):
        pltpu.make_async_remote_copy(
            src_ref=dst,
            dst_ref=dst,
            send_sem=self.send_sem.at[slot],
            recv_sem=self.recv_sem.at[slot],
            device_id=where,
            device_id_type=pl.DeviceIdType.MESH,
        ).wait_recv()

    def finish(self):
        for copy in self.made:
            copy.wait_send()


def greet(targets):
    barrier = pltpu.get_barrier_semaphore()
    for where in targets:
        pl.semaphore_signal(barrier, inc=1, device_id=where, device_id_type=pl.DeviceIdType.MESH)
    pl.semaphore_wait(barrier, len(targets))


def gather_kernel(n_group, n_dp, cuts, w_ref, g_ref, out_ref, gout_ref, send_sem, recv_sem):
    me, dp = lax.axis_index("group"), lax.axis_index("dp")
    core, chip, chips = me % 2, me // 2, n_group // 2
    sib = me + 1 - 2 * core
    half = dp % 2
    pair = dp + 1 - 2 * half
    half_rows = w_ref.shape[0] // 2
    at = lambda rank, d: {"group": rank, "dp": d}
    others = [(me + j) % n_group for j in range(1, n_group)]
    greet([at(rank, dp) for rank in others] + [at(me, pair)])
    copies = Copies(send_sem, recv_sem)
    n_cut = len(cuts)
    far = chips - 1
    base_far = 0
    base_pair = base_far + far * n_cut
    base_near = base_pair + far * n_cut
    base_near_pair = base_near + far * n_cut
    base_own = base_near_pair + far * n_cut
    base_gain = base_own + n_cut + 1
    gout_ref[pl.ds(me, 1)] = g_ref[...][None]

    def cast(start, rows):
        def step(i, block):
            out_ref[me, rows_at(start + i, block), :] = w_ref[
                rows_at(start + i, block), :
            ].astype(jnp.bfloat16)

        over_rows(rows, step)

    starts = []
    start = 0
    for rows in cuts:
        starts.append(start)
        start += rows
    mine = half * half_rows
    theirs = (1 - half) * half_rows
    for c in range(n_cut):
        cast(mine + starts[c], cuts[c])
        piece = out_ref.at[me, rows_at(mine + starts[c], cuts[c]), :]
        for j in range(1, chips):
            to = ((chip + j) % chips) * 2 + core
            copies.start(piece, piece, base_far + (j - 1) * n_cut + c, at(to, dp))
        copies.start(piece, piece, base_own + c, at(sib, dp))
    for j in range(1, n_group):
        line = gout_ref.at[me]
        copies.start(line, line, base_gain + j - 1, at((me + j) % n_group, dp))
    cast(theirs, half_rows)
    rest = out_ref.at[me, rows_at(theirs, half_rows), :]
    copies.start(rest, rest, base_own + n_cut, at(sib, dp))
    for c in range(n_cut + 1):
        for j in range(1, chips):
            source = ((chip + chips - j) % chips) * 2 + core
            if c < n_cut:
                piece = out_ref.at[source, rows_at(mine + starts[c], cuts[c]), :]
                slot = (j - 1) * n_cut + c
                copies.arrived(piece, base_far + slot, at(source, dp))
                copies.start(piece, piece, base_pair + slot, at(me, pair))
                copies.start(piece, piece, base_near + slot, at(sib, dp))
            if c > 0:
                piece = out_ref.at[source, rows_at(theirs + starts[c - 1], cuts[c - 1]), :]
                slot = (j - 1) * n_cut + c - 1
                copies.arrived(piece, base_pair + slot, at(me, pair))
                copies.start(piece, piece, base_near_pair + slot, at(sib, dp))
    for c in range(n_cut):
        piece = out_ref.at[sib, rows_at(mine + starts[c], cuts[c]), :]
        copies.arrived(piece, base_own + c, at(sib, dp))
    rest = out_ref.at[sib, rows_at(theirs, half_rows), :]
    copies.arrived(rest, base_own + n_cut, at(sib, dp))
    for j in range(1, chips):
        source = ((chip + chips - j) % chips) * 2 + (1 - core)
        for c in range(n_cut):
            slot = (j - 1) * n_cut + c
            piece = out_ref.at[source, rows_at(mine + starts[c], cuts[c]), :]
            copies.arrived(piece, base_near + slot, at(sib, dp))
            piece = out_ref.at[source, rows_at(theirs + starts[c], cuts[c]), :]
            copies.arrived(piece, base_near_pair + slot, at(sib, dp))
    for j in range(1, n_group):
        source = (me + n_group - j) % n_group
        copies.arrived(gout_ref.at[source], base_gain + j - 1, at(source, dp))
    copies.finish()


def gather_weights(weights, gains, n_group, n_dp):
    rows = weights.shape[0] // LANES
    cuts = [units * TILE for units in cut_evenly(rows // 2 // TILE, 4)]
    gain_size = gains.shape[0] * gains.shape[1]
    gain_tile = (
        jnp.zeros((TILE * LANES,), jnp.bfloat16)
        .at[:gain_size]
        .set(gains.astype(jnp.bfloat16).reshape(-1))
        .reshape(TILE, LANES)
    )
    far = n_group // 2 - 1
    slots = 4 * far * len(cuts) + len(cuts) + 1 + n_group - 1
    vmem = pl.BlockSpec(memory_space=pltpu.VMEM)
    full, full_gains = pl.pallas_call(
        functools.partial(gather_kernel, n_group, n_dp, cuts),
        out_shape=(
            jax.ShapeDtypeStruct((n_group, rows, LANES), jnp.bfloat16),
            jax.ShapeDtypeStruct((n_group, TILE, LANES), jnp.bfloat16),
        ),
        in_specs=[vmem, vmem],
        out_specs=(vmem, vmem),
        scratch_shapes=[pltpu.SemaphoreType.DMA((slots,)), pltpu.SemaphoreType.DMA((slots,))],
        compiler_params=pltpu.CompilerParams(
            collective_id=0, has_side_effects=True, vmem_limit_bytes=40 * 1024 * 1024
        ),
    )(weights.reshape(rows, LANES), gain_tile)
    full_gains = full_gains.reshape(n_group, -1)[:, :gain_size]
    full_gains = full_gains.reshape(n_group, gains.shape[0], gains.shape[1])
    return full.reshape(-1), full_gains.transpose(1, 0, 2).reshape(gains.shape[0], -1)


def reduce_kernel(
    n_group, n_dp, cuts, main_rows, src_ref, tail_ref, out_ref,
    buf1, buf2, sum2, buf3, sum3, buf4, send_sem, recv_sem,
):
    me, dp = lax.axis_index("group"), lax.axis_index("dp")
    core, chip, chips = me % 2, me // 2, n_group // 2
    sib = me + 1 - 2 * core
    half = dp % 2
    pair = dp + 1 - 2 * half
    place, places = dp // 2, n_dp // 2
    at = lambda rank, d: {"group": rank, "dp": d}
    far_to = [((chip + j) % chips) * 2 + core for j in range(1, chips)]
    line_to = [((place + j) % places) * 2 + half for j in range(1, places)]
    greet(
        [at(sib, dp)] + [at(rank, dp) for rank in far_to]
        + [at(me, pair)] + [at(me, d) for d in line_to]
    )
    copies = Copies(send_sem, recv_sem)
    per = 3 + (chips - 1) + 2 * (places - 1)
    f32 = jnp.float32
    starts = []
    start = 0
    for rows in cuts:
        starts.append(start)
        start += rows

    def source(c):
        if starts[c] < main_rows:
            return src_ref, starts[c]
        return tail_ref, starts[c] - main_rows

    def send_core(c):
        ref, off = source(c)
        rows = cuts[c]
        copies.start(
            ref.at[:, 1 - core, pl.ds(off, rows), :],
            buf1.at[:, pl.ds(starts[c], rows), :],
            c * per,
            at(sib, dp),
        )

    def after_core(c):
        ref, off = source(c)
        rows, o = cuts[c], starts[c]
        copies.arrived(buf1.at[:, pl.ds(o, rows), :], c * per, at(sib, dp))
        for j in range(1, chips):
            k = (chip + j) % chips

            def step(i, block):
                here = rows_at(o + i, block)
                total = buf1[k, here, :].astype(f32) + ref[
                    k, core, rows_at(off + i, block), :
                ].astype(f32)
                buf1[k, here, :] = total.astype(jnp.bfloat16)

            over_rows(rows, step)
            copies.start(
                buf1.at[k, pl.ds(o, rows), :],
                buf2.at[j - 1, pl.ds(o, rows), :],
                c * per + j,
                at(far_to[j - 1], dp),
            )

    def after_far(c):
        ref, off = source(c)
        rows, o = cuts[c], starts[c]
        for j in range(1, chips):
            copies.arrived(buf2.at[j - 1, pl.ds(o, rows), :], c * per + j, at(far_to[j - 1], dp))

        def step(i, block):
            here = rows_at(o + i, block)
            total = buf1[chip, here, :].astype(f32) + ref[
                chip, core, rows_at(off + i, block), :
            ].astype(f32)
            for j in range(1, chips):
                total = total + buf2[j - 1, here, :].astype(f32)
            sum2[here, :] = total.astype(jnp.bfloat16)

        over_rows(rows, step)
        part = rows // 2
        copies.start(
            sum2.at[rows_at(o + (1 - half) * part, part), :],
            buf3.at[pl.ds(o // 2, part), :],
            c * per + chips,
            at(me, pair),
        )

    def after_pair(c):
        part, o = cuts[c] // 2, starts[c]
        copies.arrived(buf3.at[pl.ds(o // 2, part), :], c * per + chips, at(me, pair))

        def step(i, block):
            here = rows_at(o // 2 + i, block)
            total = sum2[rows_at(o + half * part + i, block), :].astype(f32)
            sum3[here, :] = (total + buf3[here, :].astype(f32)).astype(jnp.bfloat16)

        over_rows(part, step)
        piece = part // places
        for j in range(1, places):
            to = (place + j) % places
            copies.start(
                sum3.at[rows_at(o // 2 + to * piece, piece), :],
                buf4.at[j - 1, pl.ds(o // n_dp, piece), :],
                c * per + chips + j,
                at(me, line_to[j - 1]),
            )

    def after_line(c):
        part, o = cuts[c] // 2, starts[c]
        piece = part // places
        for j in range(1, places):
            copies.arrived(
                buf4.at[j - 1, pl.ds(o // n_dp, piece), :],
                c * per + chips + j,
                at(me, line_to[j - 1]),
            )
        first = o + half * part + place * piece

        def step(i, block):
            total = sum3[rows_at(o // 2 + place * piece + i, block), :].astype(f32)
            for j in range(1, places):
                total = total + buf4[j - 1, rows_at(o // n_dp + i, block), :].astype(f32)
            out_ref[rows_at(first + i, block), :] = total.astype(jnp.bfloat16)

        over_rows(piece, step)
        done = out_ref.at[rows_at(first, piece), :]
        for j in range(1, places):
            copies.start(done, done, c * per + chips + places - 1 + j, at(me, line_to[j - 1]))

    def after_back(c):
        part, o = cuts[c] // 2, starts[c]
        piece = part // places
        for j in range(1, places):
            origin = (place + places - j) % places
            copies.arrived(
                out_ref.at[rows_at(o + half * part + origin * piece, piece), :],
                c * per + chips + places - 1 + j,
                at(me, line_to[j - 1]),
            )
        done = out_ref.at[rows_at(o + half * part, part), :]
        copies.start(done, done, c * per + per - 1, at(me, pair))

    def last(c):
        part, o = cuts[c] // 2, starts[c]
        copies.arrived(
            out_ref.at[rows_at(o + (1 - half) * part, part), :], c * per + per - 1, at(me, pair)
        )

    n_cut = len(cuts)
    for c in range(n_cut):
        send_core(c)
    stages = [after_core, after_far, after_pair, after_line, after_back, last]
    lags = [0, 2, 3, 4, 5, 6]
    for t in range(n_cut + lags[-1]):
        for stage, lag in zip(stages, lags):
            if 0 <= t - lag < n_cut:
                stage(t - lag)
    copies.finish()


def reduce_grads(flat_grad, gain_grad, n_group, n_dp):
    shard_rows = flat_grad.shape[0] // n_group // LANES
    unit = TILE * n_dp
    main_units = shard_rows // unit
    main_rows = main_units * unit
    spare = shard_rows - main_rows
    gain_cols = gain_grad.shape[1] // n_group
    gain_size = gain_grad.shape[0] * gain_cols
    gain_flat = gain_grad.reshape(-1, n_group, gain_cols).transpose(1, 0, 2).reshape(n_group, -1)
    gain_rows = -(-gain_size // LANES)
    tail_rows = -(-(spare + gain_rows) // unit) * unit
    gain_flat = jnp.pad(gain_flat, ((0, 0), (0, (tail_rows - spare) * LANES - gain_size)))
    main = flat_grad.reshape(n_group, shard_rows, LANES)
    tail = gain_flat.reshape(n_group, tail_rows - spare, LANES)
    if spare:
        tail = jnp.concatenate([main[:, main_rows:], tail], axis=1)
    cuts = [units * unit for units in cut_evenly(main_units, 6)] + [tail_rows]
    total_rows = main_rows + tail_rows
    chips, places = n_group // 2, n_dp // 2
    slots = len(cuts) * (3 + (chips - 1) + 2 * (places - 1))
    vmem = pl.BlockSpec(memory_space=pltpu.VMEM)
    bf16 = jnp.bfloat16
    out = pl.pallas_call(
        functools.partial(reduce_kernel, n_group, n_dp, cuts, main_rows),
        out_shape=jax.ShapeDtypeStruct((total_rows, LANES), bf16),
        in_specs=[vmem, vmem],
        out_specs=vmem,
        scratch_shapes=[
            pltpu.VMEM((chips, total_rows, LANES), bf16),
            pltpu.VMEM((chips - 1, total_rows, LANES), bf16),
            pltpu.VMEM((total_rows, LANES), bf16),
            pltpu.VMEM((total_rows // 2, LANES), bf16),
            pltpu.VMEM((total_rows // 2, LANES), bf16),
            pltpu.VMEM((places - 1, total_rows // n_dp, LANES), bf16),
            pltpu.SemaphoreType.DMA((slots,)),
            pltpu.SemaphoreType.DMA((slots,)),
        ],
        compiler_params=pltpu.CompilerParams(
            collective_id=1, has_side_effects=True, vmem_limit_bytes=40 * 1024 * 1024
        ),
    )(
        main.reshape(chips, 2, shard_rows, LANES),
        tail.reshape(chips, 2, tail_rows, LANES),
    )
    grad_shard = out[:shard_rows].reshape(-1).astype(jnp.float32)
    gain_shard = out[shard_rows : shard_rows + gain_rows].reshape(-1)[:gain_size]
    return grad_shard, gain_shard.reshape(-1, gain_cols).astype(jnp.float32)


def body(
    n_group,
    n_dp,
    hidden_in,
    out_grad,
    span_order,
    weights,
    first_moment,
    second_moment,
    gains,
    gain_first,
    gain_second,
):
    group_rank = lax.axis_index("group")
    seq_local = hidden_in.shape[0]
    slot_len = hidden_in.shape[1]
    width = hidden_in.shape[2]
    q_width = HEADS * HEAD_DIM
    kv_width = KV_HEADS * HEAD_DIM
    group_size = HEADS // KV_HEADS
    full_flat, full_gains = gather_weights(weights, gains, n_group, n_dp)
    w_query, w_key, w_value, w_out, w_gate, w_up, w_down = split_weights(full_flat)
    gain_attn = full_gains[0].astype(jnp.float32)
    gain_ffn = full_gains[1].astype(jnp.float32)
    offsets = jnp.arange(SPAN, dtype=jnp.int32)
    all_pos = (span_order[:, :, None] * SPAN + offsets[None, None, :]).reshape(seq_local, -1)
    local_pos = lax.dynamic_slice_in_dim(all_pos, group_rank * slot_len, slot_len, 1)
    cosine, sine_table = rope_tables(local_pos.reshape(-1))
    residual = hidden_in.reshape(-1, width).astype(jnp.float32)
    normed_one, factor_one = norm_forward(residual)
    attn_in = (normed_one * gain_attn).astype(jnp.bfloat16)
    query_proj = jnp.dot(attn_in, w_query, preferred_element_type=jnp.float32).reshape(
        -1, HEADS, HEAD_DIM
    )
    key_proj = jnp.dot(attn_in, w_key, preferred_element_type=jnp.float32).reshape(
        -1, KV_HEADS, HEAD_DIM
    )
    value_proj = jnp.dot(attn_in, w_value, preferred_element_type=jnp.float32)
    query_b = rotate(query_proj, cosine, sine_table).astype(jnp.bfloat16)
    key_b = rotate(key_proj, cosine, sine_table).astype(jnp.bfloat16).reshape(-1, kv_width)
    value_b = value_proj.astype(jnp.bfloat16)
    kv_local = jnp.concatenate([key_b, value_b], axis=-1).reshape(seq_local, slot_len, 2 * kv_width)
    kv_all = lax.all_gather(kv_local, "group", axis=1, tiled=True)
    query_seq = query_b.reshape(seq_local, slot_len, KV_HEADS, group_size, HEAD_DIM)
    attn_parts = []
    lse_parts = []
    for seq_index in range(seq_local):
        attn_one, lse_one = attend(
            query_seq[seq_index], kv_all[seq_index], local_pos[seq_index], all_pos[seq_index]
        )
        attn_parts.append(attn_one)
        lse_parts.append(lse_one)
    attn_b = jnp.concatenate(attn_parts, axis=0)
    middle = residual + jnp.dot(attn_b, w_out, preferred_element_type=jnp.float32)
    normed_two, factor_two = norm_forward(middle)
    ffn_in = (normed_two * gain_ffn).astype(jnp.bfloat16)
    gate_proj = jnp.dot(ffn_in, w_gate, preferred_element_type=jnp.float32)
    up_proj = jnp.dot(ffn_in, w_up, preferred_element_type=jnp.float32)
    sigmoid_gate = jax.nn.sigmoid(gate_proj)
    hidden = (gate_proj * sigmoid_gate * up_proj).astype(jnp.bfloat16)
    block_out = middle + jnp.dot(hidden, w_down, preferred_element_type=jnp.float32)
    grad_out = out_grad.reshape(-1, width)
    gw_down = outer_sum(hidden, grad_out)
    grad_hidden = jnp.dot(grad_out, w_down.T, preferred_element_type=jnp.float32)
    grad_gate = (
        grad_hidden * up_proj * sigmoid_gate * (1.0 + gate_proj * (1.0 - sigmoid_gate))
    ).astype(jnp.bfloat16)
    grad_up = (grad_hidden * gate_proj * sigmoid_gate).astype(jnp.bfloat16)
    gw_gate = outer_sum(ffn_in, grad_gate)
    gw_up = outer_sum(ffn_in, grad_up)
    grad_ffn_in = jnp.dot(grad_gate, w_gate.T, preferred_element_type=jnp.float32) + jnp.dot(
        grad_up, w_up.T, preferred_element_type=jnp.float32
    )
    gg_ffn = jnp.sum(grad_ffn_in * normed_two, axis=0)
    grad_middle = grad_out.astype(jnp.float32) + norm_backward(
        grad_ffn_in * gain_ffn, normed_two, factor_two
    )
    grad_middle_b = grad_middle.astype(jnp.bfloat16)
    gw_out = outer_sum(attn_b, grad_middle_b)
    grad_attn = jnp.dot(grad_middle_b, w_out.T, preferred_element_type=jnp.float32).astype(
        jnp.bfloat16
    )
    kv_back = lax.all_gather(kv_local, "group", axis=1, tiled=True)
    attn_seq = attn_b.reshape(seq_local, slot_len, q_width)
    grad_attn_seq = grad_attn.reshape(seq_local, slot_len, q_width)
    query_grads = []
    kv_grads = []
    for seq_index in range(seq_local):
        grad_query_one, grad_kv_one = attend_back(
            query_seq[seq_index],
            kv_back[seq_index],
            local_pos[seq_index],
            all_pos[seq_index],
            lse_parts[seq_index],
            attn_seq[seq_index],
            grad_attn_seq[seq_index],
        )
        query_grads.append(grad_query_one)
        kv_grads.append(grad_kv_one)
    grad_query = jnp.concatenate(query_grads, axis=0).reshape(-1, HEADS, HEAD_DIM)
    grad_kv_all = jnp.stack(kv_grads)
    grad_kv = lax.psum_scatter(grad_kv_all, "group", scatter_dimension=1, tiled=True).reshape(
        -1, 2 * kv_width
    )
    grad_query_b = (
        rotate_back(grad_query, cosine, sine_table).reshape(-1, q_width).astype(jnp.bfloat16)
    )
    grad_key_b = (
        rotate_back(grad_kv[:, :kv_width].reshape(-1, KV_HEADS, HEAD_DIM), cosine, sine_table)
        .reshape(-1, kv_width)
        .astype(jnp.bfloat16)
    )
    grad_value_b = grad_kv[:, kv_width:].astype(jnp.bfloat16)
    gw_query = outer_sum(attn_in, grad_query_b)
    gw_key = outer_sum(attn_in, grad_key_b)
    gw_value = outer_sum(attn_in, grad_value_b)
    grad_attn_in = jnp.dot(grad_query_b, w_query.T, preferred_element_type=jnp.float32)
    grad_attn_in = grad_attn_in + jnp.dot(grad_key_b, w_key.T, preferred_element_type=jnp.float32)
    grad_attn_in = grad_attn_in + jnp.dot(
        grad_value_b, w_value.T, preferred_element_type=jnp.float32
    )
    gg_attn = jnp.sum(grad_attn_in * normed_one, axis=0)
    in_grad = grad_middle + norm_backward(grad_attn_in * gain_attn, normed_one, factor_one)
    flat_grad = jnp.concatenate(
        [
            grad_item.reshape(-1)
            for grad_item in (gw_query, gw_key, gw_value, gw_out, gw_gate, gw_up, gw_down)
        ]
    )
    gain_grad = jnp.stack([gg_attn, gg_ffn])
    grad_shard, gain_shard = reduce_grads(
        flat_grad.astype(jnp.bfloat16), gain_grad.astype(jnp.bfloat16), n_group, n_dp
    )
    new_weights, new_first, new_second = adamw_step(
        weights, first_moment, second_moment, grad_shard, DECAY_RATE, LEARN_RATE
    )
    new_gains, new_gain_first, new_gain_second = adamw_step(
        gains, gain_first, gain_second, gain_shard, 0.0, GAIN_RATE
    )
    return (
        block_out.reshape(seq_local, slot_len, width),
        in_grad.reshape(seq_local, slot_len, width),
        grad_shard,
        gain_shard,
        new_weights,
        new_first,
        new_second,
        new_gains,
        new_gain_first,
        new_gain_second,
    )


def solution(mesh):
    in_specs = (
        P("dp", "group", None),
        P("dp", "group", None),
        P("dp", None),
        P("group"),
        P("group"),
        P("group"),
        P(None, "group"),
        P(None, "group"),
        P(None, "group"),
    )
    out_specs = (
        P("dp", "group", None),
        P("dp", "group", None),
        P("group"),
        P(None, "group"),
        P("group"),
        P("group"),
        P("group"),
        P(None, "group"),
        P(None, "group"),
        P(None, "group"),
    )
    return jax.shard_map(
        functools.partial(body, mesh.shape["group"], mesh.shape["dp"]),
        mesh=mesh, in_specs=in_specs, out_specs=out_specs, check_vma=False)
```

```python
import functools

import jax
import jax.numpy as jnp
from jax import lax
from jax.experimental import pallas as pl
from jax.experimental.pallas import tpu as pltpu
from jax.sharding import PartitionSpec as P

D = 576
HEADS = 9
KV_HEADS = 3
HEAD_DIM = 64
FF = 1536
SPAN = 32


EPS_NORM = 1e-05
ROPE_BASE = 100000.0
BETA_ONE = 0.9
BETA_TWO = 0.95
LEARN_RATE = 0.02
GAIN_RATE = 0.25
DECAY_RATE = 0.1
EPS_ADAM = 1e-08
CORRECT_ONE = 1.0 - 0.9**5
CORRECT_TWO = 1.0 - 0.95**5
NEG_LARGE = -1e30
LANES = 128
TILE = 16


def split_weights(flat_vector):
    q_width = HEADS * HEAD_DIM
    kv_width = KV_HEADS * HEAD_DIM
    layout = [(D, q_width), (D, kv_width), (D, kv_width), (q_width, D), (D, FF), (D, FF), (FF, D)]
    pieces = []
    offset = 0
    for rows_cols in layout:
        amount = rows_cols[0] * rows_cols[1]
        piece = lax.slice_in_dim(
            flat_vector, offset // LANES, (offset + amount) // LANES, axis=0
        )
        pieces.append(lax.optimization_barrier(piece).reshape(rows_cols))
        offset = offset + amount
    return pieces


def rope_tables(positions):
    freq_index = jnp.arange(HEAD_DIM // 2, dtype=jnp.float32)
    inverse = ROPE_BASE ** (-2.0 * freq_index / HEAD_DIM)
    angles = positions.astype(jnp.float32)[:, None] * inverse[None, :]
    return (jnp.cos(angles), jnp.sin(angles))


def rotate(vectors, cosine, sine_table):
    half_dim = HEAD_DIM // 2
    first_half = vectors[..., :half_dim]
    second_half = vectors[..., half_dim:]
    cos_b = cosine[:, None, :]
    sin_b = sine_table[:, None, :]
    return jnp.concatenate(
        [first_half * cos_b - second_half * sin_b, second_half * cos_b + first_half * sin_b],
        axis=-1,
    )


def rotate_back(vectors, cosine, sine_table):
    half_dim = HEAD_DIM // 2
    first_half = vectors[..., :half_dim]
    second_half = vectors[..., half_dim:]
    cos_b = cosine[:, None, :]
    sin_b = sine_table[:, None, :]
    return jnp.concatenate(
        [first_half * cos_b + second_half * sin_b, second_half * cos_b - first_half * sin_b],
        axis=-1,
    )


def norm_forward(vectors):
    factor = lax.rsqrt(jnp.mean(vectors * vectors, axis=-1, keepdims=True) + EPS_NORM)
    return (vectors * factor, factor)


def norm_backward(grad_normed, normed, factor):
    return factor * (grad_normed - normed * jnp.mean(grad_normed * normed, axis=-1, keepdims=True))


def outer_sum(left_rows, right_rows):
    return lax.dot_general(
        left_rows, right_rows, (((0,), (0,)), ((), ())), preferred_element_type=jnp.float32
    )


def adamw_step(param_now, moment_one, moment_two, grad_now, decay_weight, step_rate):
    first_new = BETA_ONE * moment_one + (1.0 - BETA_ONE) * grad_now
    second_new = BETA_TWO * moment_two + (1.0 - BETA_TWO) * grad_now * grad_now
    update = first_new / CORRECT_ONE / (jnp.sqrt(second_new / CORRECT_TWO) + EPS_ADAM)
    return (param_now - step_rate * (update + decay_weight * param_now), first_new, second_new)


def split_pair(kv_seq):
    kv_width = KV_HEADS * HEAD_DIM
    key_blk = kv_seq[:, :kv_width].reshape(-1, KV_HEADS, HEAD_DIM)
    value_blk = kv_seq[:, kv_width:].reshape(-1, KV_HEADS, HEAD_DIM)
    return (key_blk, value_blk)


def masked_scores(query_blk, key_blk, query_pos, key_pos):
    scores = jnp.einsum(
        "qkgd,skd->kgqs", query_blk, key_blk, preferred_element_type=jnp.float32
    ) * HEAD_DIM ** (-0.5)
    allowed = key_pos[None, :] <= query_pos[:, None]
    return jnp.where(allowed[None, None], scores, NEG_LARGE)


def attend(query_blk, kv_seq, query_pos, key_pos):
    key_blk, value_blk = split_pair(kv_seq)
    scores = masked_scores(query_blk, key_blk, query_pos, key_pos)
    row_max = jnp.max(scores, axis=-1)
    log_total = row_max + jnp.log(jnp.sum(jnp.exp(scores - row_max[..., None]), axis=-1))
    probs_b = jnp.exp(scores - log_total[..., None]).astype(jnp.bfloat16)
    attn_vals = jnp.einsum("kgqs,skd->qkgd", probs_b, value_blk, preferred_element_type=jnp.float32)
    return (attn_vals.reshape(attn_vals.shape[0], -1).astype(jnp.bfloat16), log_total)


def attend_back(query_blk, kv_seq, query_pos, key_pos, log_total, attn_rows, grad_rows):
    group_size = HEADS // KV_HEADS
    key_blk, value_blk = split_pair(kv_seq)
    scores = masked_scores(query_blk, key_blk, query_pos, key_pos)
    probs = jnp.exp(scores - log_total[..., None])
    probs_b = probs.astype(jnp.bfloat16)
    grad_heads = grad_rows.reshape(-1, KV_HEADS, group_size, HEAD_DIM)
    attn_heads = attn_rows.reshape(-1, KV_HEADS, group_size, HEAD_DIM)
    delta_rows = jnp.einsum(
        "qkgd,qkgd->kgq", grad_heads, attn_heads, preferred_element_type=jnp.float32
    )
    grad_probs = jnp.einsum(
        "qkgd,skd->kgqs", grad_heads, value_blk, preferred_element_type=jnp.float32
    )
    grad_scores = (probs * (grad_probs - delta_rows[..., None]) * HEAD_DIM ** (-0.5)).astype(
        jnp.bfloat16
    )
    grad_query = jnp.einsum(
        "kgqs,skd->qkgd", grad_scores, key_blk, preferred_element_type=jnp.float32
    )
    grad_key = jnp.einsum(
        "kgqs,qkgd->skd", grad_scores, query_blk, preferred_element_type=jnp.float32
    )
    grad_value = jnp.einsum(
        "kgqs,qkgd->skd", probs_b, grad_heads, preferred_element_type=jnp.float32
    )
    key_rows = grad_key.shape[0]
    stacked = jnp.concatenate(
        [grad_key.reshape(key_rows, -1), grad_value.reshape(key_rows, -1)], axis=-1
    )
    return (grad_query, stacked)


def cut_evenly(total_units, most):
    count = max(1, min(most, total_units))
    base, extra = divmod(total_units, count)
    return [base + (1 if i < extra else 0) for i in range(count)]


def block_of(rows):
    for block in (144, 128, 96, 64, 48, 32):
        if rows % block == 0:
            return block
    return TILE


def over_rows(rows, step):
    block = block_of(rows)
    if rows == block:
        step(0, block)
        return

    def one(i, carry):
        step(pl.multiple_of(i * block, TILE), block)
        return carry

    lax.fori_loop(0, rows // block, one, 0)


def rows_at(start, size):
    return pl.ds(start if isinstance(start, int) else pl.multiple_of(start, TILE), size)


class Copies:
    def __init__(self, send_sem, recv_sem):
        self.send_sem, self.recv_sem, self.made = send_sem, recv_sem, []

    def start(self, src, dst, slot, where):
        copy = pltpu.make_async_remote_copy(
            src_ref=src,
            dst_ref=dst,
            send_sem=self.send_sem.at[slot],
            recv_sem=self.recv_sem.at[slot],
            device_id=where,
            device_id_type=pl.DeviceIdType.MESH,
        )
        copy.start()
        self.made.append(copy)

    def arrived(self, dst, slot, where):
        pltpu.make_async_remote_copy(
            src_ref=dst,
            dst_ref=dst,
            send_sem=self.send_sem.at[slot],
            recv_sem=self.recv_sem.at[slot],
            device_id=where,
            device_id_type=pl.DeviceIdType.MESH,
        ).wait_recv()

    def finish(self):
        for copy in self.made:
            copy.wait_send()


def greet(targets):
    barrier = pltpu.get_barrier_semaphore()
    for where in targets:
        pl.semaphore_signal(barrier, inc=1, device_id=where, device_id_type=pl.DeviceIdType.MESH)
    pl.semaphore_wait(barrier, len(targets))


def gather_kernel(n_group, n_dp, cuts, w_ref, g_ref, out_ref, gout_ref, send_sem, recv_sem):
    me, dp = lax.axis_index("group"), lax.axis_index("dp")
    core, chip, chips = me % 2, me // 2, n_group // 2
    sib = me + 1 - 2 * core
    half = dp % 2
    pair = dp + 1 - 2 * half
    half_rows = w_ref.shape[0] // 2
    at = lambda rank, d: {"group": rank, "dp": d}
    others = [(me + j) % n_group for j in range(1, n_group)]
    greet([at(rank, dp) for rank in others] + [at(me, pair)])
    copies = Copies(send_sem, recv_sem)
    n_cut = len(cuts)
    far = chips - 1
    base_far = 0
    base_pair = base_far + far * n_cut
    base_near = base_pair + far * n_cut
    base_near_pair = base_near + far * n_cut
    base_own = base_near_pair + far * n_cut
    base_gain = base_own + n_cut + 1
    gout_ref[pl.ds(me, 1)] = g_ref[...][None]

    def cast(start, rows):
        def step(i, block):
            out_ref[me, rows_at(start + i, block), :] = w_ref[
                rows_at(start + i, block), :
            ].astype(jnp.bfloat16)

        over_rows(rows, step)

    starts = []
    start = 0
    for rows in cuts:
        starts.append(start)
        start += rows
    mine = half * half_rows
    theirs = (1 - half) * half_rows
    for c in range(n_cut):
        cast(mine + starts[c], cuts[c])
        piece = out_ref.at[me, rows_at(mine + starts[c], cuts[c]), :]
        for j in range(1, chips):
            to = ((chip + j) % chips) * 2 + core
            copies.start(piece, piece, base_far + (j - 1) * n_cut + c, at(to, dp))
        copies.start(piece, piece, base_own + c, at(sib, dp))
    for j in range(1, n_group):
        line = gout_ref.at[me]
        copies.start(line, line, base_gain + j - 1, at((me + j) % n_group, dp))
    cast(theirs, half_rows)
    rest = out_ref.at[me, rows_at(theirs, half_rows), :]
    copies.start(rest, rest, base_own + n_cut, at(sib, dp))
    for c in range(n_cut + 1):
        for j in range(1, chips):
            source = ((chip + chips - j) % chips) * 2 + core
            if c < n_cut:
                piece = out_ref.at[source, rows_at(mine + starts[c], cuts[c]), :]
                slot = (j - 1) * n_cut + c
                copies.arrived(piece, base_far + slot, at(source, dp))
                copies.start(piece, piece, base_pair + slot, at(me, pair))
                copies.start(piece, piece, base_near + slot, at(sib, dp))
            if c > 0:
                piece = out_ref.at[source, rows_at(theirs + starts[c - 1], cuts[c - 1]), :]
                slot = (j - 1) * n_cut + c - 1
                copies.arrived(piece, base_pair + slot, at(me, pair))
                copies.start(piece, piece, base_near_pair + slot, at(sib, dp))
    for c in range(n_cut):
        piece = out_ref.at[sib, rows_at(mine + starts[c], cuts[c]), :]
        copies.arrived(piece, base_own + c, at(sib, dp))
    rest = out_ref.at[sib, rows_at(theirs, half_rows), :]
    copies.arrived(rest, base_own + n_cut, at(sib, dp))
    for j in range(1, chips):
        source = ((chip + chips - j) % chips) * 2 + (1 - core)
        for c in range(n_cut):
            slot = (j - 1) * n_cut + c
            piece = out_ref.at[source, rows_at(mine + starts[c], cuts[c]), :]
            copies.arrived(piece, base_near + slot, at(sib, dp))
            piece = out_ref.at[source, rows_at(theirs + starts[c], cuts[c]), :]
            copies.arrived(piece, base_near_pair + slot, at(sib, dp))
    for j in range(1, n_group):
        source = (me + n_group - j) % n_group
        copies.arrived(gout_ref.at[source], base_gain + j - 1, at(source, dp))
    copies.finish()


def gather_weights(weights, gains, n_group, n_dp):
    rows = weights.shape[0] // LANES
    cuts = [units * TILE for units in cut_evenly(rows // 2 // TILE, 4)]
    gain_size = gains.shape[0] * gains.shape[1]
    gain_tile = (
        jnp.zeros((TILE * LANES,), jnp.bfloat16)
        .at[:gain_size]
        .set(gains.astype(jnp.bfloat16).reshape(-1))
        .reshape(TILE, LANES)
    )
    far = n_group // 2 - 1
    slots = 4 * far * len(cuts) + len(cuts) + 1 + n_group - 1
    vmem = pl.BlockSpec(memory_space=pltpu.VMEM)
    full, full_gains = pl.pallas_call(
        functools.partial(gather_kernel, n_group, n_dp, cuts),
        out_shape=(
            jax.ShapeDtypeStruct((n_group, rows, LANES), jnp.bfloat16),
            jax.ShapeDtypeStruct((n_group, TILE, LANES), jnp.bfloat16),
        ),
        in_specs=[vmem, vmem],
        out_specs=(vmem, vmem),
        scratch_shapes=[pltpu.SemaphoreType.DMA((slots,)), pltpu.SemaphoreType.DMA((slots,))],
        compiler_params=pltpu.CompilerParams(
            collective_id=0, has_side_effects=True, vmem_limit_bytes=16 * 1024 * 1024
        ),
    )(weights.reshape(rows, LANES), gain_tile)
    full_gains = full_gains.reshape(n_group, -1)[:, :gain_size]
    full_gains = full_gains.reshape(n_group, gains.shape[0], gains.shape[1])
    return full.reshape(-1, LANES), full_gains.transpose(1, 0, 2).reshape(gains.shape[0], -1)


def reduce_kernel(n_group, n_dp, cuts, moves, *refs):
    pieces = refs[: 1 + max(move[0] for move in moves)]
    (gain_ref, out_ref, src, buf1, buf2, sum2, buf3, sum3, buf4, send_sem, recv_sem, local_sem) = refs[
        len(pieces) :
    ]
    me, dp = lax.axis_index("group"), lax.axis_index("dp")
    core, chip, chips = me % 2, me // 2, n_group // 2
    sib = me + 1 - 2 * core
    half = dp % 2
    pair = dp + 1 - 2 * half
    place, places = dp // 2, n_dp // 2
    at = lambda rank, d: {"group": rank, "dp": d}
    far_to = [((chip + j) % chips) * 2 + core for j in range(1, chips)]
    line_to = [((place + j) % places) * 2 + half for j in range(1, places)]
    local = []
    for number, (piece, first, rank, row, rows) in enumerate(moves):
        local.append(
            pltpu.make_async_copy(
                pieces[piece].at[pl.ds(first, rows), :],
                src.at[rank // 2, rank % 2, pl.ds(row, rows), :],
                local_sem.at[number],
            )
        )
    gain_rows = gain_ref.shape[2]
    local.append(
        pltpu.make_async_copy(
            gain_ref,
            src.at[:, :, pl.ds(src.shape[2] - gain_rows, gain_rows), :],
            local_sem.at[len(moves)],
        )
    )
    for copy in local:
        copy.start()
    greet(
        [at(sib, dp)] + [at(rank, dp) for rank in far_to]
        + [at(me, pair)] + [at(me, d) for d in line_to]
    )
    copies = Copies(send_sem, recv_sem)
    per = 3 + (chips - 1) + 2 * (places - 1)
    f32 = jnp.float32
    starts = [start for start, _ in cuts]
    cuts = [rows for _, rows in cuts]
    for copy in local:
        copy.wait()

    def send_core(c):
        rows = cuts[c]
        copies.start(
            src.at[:, 1 - core, pl.ds(starts[c], rows), :],
            buf1.at[:, pl.ds(starts[c], rows), :],
            c * per,
            at(sib, dp),
        )

    def after_core(c):
        rows, o = cuts[c], starts[c]
        copies.arrived(buf1.at[:, pl.ds(o, rows), :], c * per, at(sib, dp))
        for j in range(1, chips):
            k = (chip + j) % chips

            def step(i, block):
                here = rows_at(o + i, block)
                total = buf1[k, here, :].astype(f32) + src[k, core, here, :].astype(f32)
                buf1[k, here, :] = total.astype(jnp.bfloat16)

            over_rows(rows, step)
            copies.start(
                buf1.at[k, pl.ds(o, rows), :],
                buf2.at[j - 1, pl.ds(o, rows), :],
                c * per + j,
                at(far_to[j - 1], dp),
            )

    def after_far(c):
        rows, o = cuts[c], starts[c]
        for j in range(1, chips):
            copies.arrived(buf2.at[j - 1, pl.ds(o, rows), :], c * per + j, at(far_to[j - 1], dp))

        def step(i, block):
            here = rows_at(o + i, block)
            total = buf1[chip, here, :].astype(f32) + src[chip, core, here, :].astype(f32)
            for j in range(1, chips):
                total = total + buf2[j - 1, here, :].astype(f32)
            sum2[here, :] = total.astype(jnp.bfloat16)

        over_rows(rows, step)
        part = rows // 2
        copies.start(
            sum2.at[rows_at(o + (1 - half) * part, part), :],
            buf3.at[pl.ds(o // 2, part), :],
            c * per + chips,
            at(me, pair),
        )

    def after_pair(c):
        part, o = cuts[c] // 2, starts[c]
        copies.arrived(buf3.at[pl.ds(o // 2, part), :], c * per + chips, at(me, pair))

        def step(i, block):
            here = rows_at(o // 2 + i, block)
            total = sum2[rows_at(o + half * part + i, block), :].astype(f32)
            sum3[here, :] = (total + buf3[here, :].astype(f32)).astype(jnp.bfloat16)

        over_rows(part, step)
        piece = part // places
        for j in range(1, places):
            to = (place + j) % places
            copies.start(
                sum3.at[rows_at(o // 2 + to * piece, piece), :],
                buf4.at[j - 1, pl.ds(o // n_dp, piece), :],
                c * per + chips + j,
                at(me, line_to[j - 1]),
            )

    def after_line(c):
        part, o = cuts[c] // 2, starts[c]
        piece = part // places
        for j in range(1, places):
            copies.arrived(
                buf4.at[j - 1, pl.ds(o // n_dp, piece), :],
                c * per + chips + j,
                at(me, line_to[j - 1]),
            )
        first = o + half * part + place * piece

        def step(i, block):
            total = sum3[rows_at(o // 2 + place * piece + i, block), :].astype(f32)
            for j in range(1, places):
                total = total + buf4[j - 1, rows_at(o // n_dp + i, block), :].astype(f32)
            out_ref[rows_at(first + i, block), :] = total.astype(jnp.bfloat16)

        over_rows(piece, step)
        done = out_ref.at[rows_at(first, piece), :]
        for j in range(1, places):
            copies.start(done, done, c * per + chips + places - 1 + j, at(me, line_to[j - 1]))

    def after_back(c):
        part, o = cuts[c] // 2, starts[c]
        piece = part // places
        for j in range(1, places):
            origin = (place + places - j) % places
            copies.arrived(
                out_ref.at[rows_at(o + half * part + origin * piece, piece), :],
                c * per + chips + places - 1 + j,
                at(me, line_to[j - 1]),
            )
        done = out_ref.at[rows_at(o + half * part, part), :]
        copies.start(done, done, c * per + per - 1, at(me, pair))

    def last(c):
        part, o = cuts[c] // 2, starts[c]
        copies.arrived(
            out_ref.at[rows_at(o + (1 - half) * part, part), :], c * per + per - 1, at(me, pair)
        )

    n_cut = len(cuts)
    for c in range(n_cut):
        send_core(c)
    stages = [after_core, after_far, after_pair, after_line, after_back, last]
    lags = [0, 2, 3, 4, 5, 6]
    for t in range(n_cut + lags[-1]):
        for stage, lag in zip(stages, lags):
            if 0 <= t - lag < n_cut:
                stage(t - lag)
    copies.finish()


def taper(total_units):
    cap = -(-total_units // 6)
    sizes = []
    while total_units:
        size = min(total_units, max(3, min(cap, total_units // 3)))
        sizes.append(size)
        total_units -= size
    return sizes


def reduce_grads(weight_parts, gain_grad, n_group, n_dp):
    pieces = [part.astype(jnp.bfloat16).reshape(-1, LANES) for part in weight_parts]
    shard_rows = sum(piece.shape[0] for piece in pieces) // n_group
    unit = TILE * n_dp
    main_units = shard_rows // unit
    main_rows = main_units * unit
    spare = shard_rows - main_rows
    gain_cols = gain_grad.shape[1] // n_group
    gain_size = gain_grad.shape[0] * gain_cols
    gain_flat = gain_grad.reshape(-1, n_group, gain_cols).transpose(1, 0, 2).reshape(n_group, -1)
    gain_rows = -(-gain_size // LANES)
    tail_rows = -(-(spare + gain_rows) // unit) * unit
    gain_flat = jnp.pad(gain_flat, ((0, 0), (0, (tail_rows - spare) * LANES - gain_size)))
    total_rows = main_rows + tail_rows
    chips, places = n_group // 2, n_dp // 2
    cuts = [(main_rows, tail_rows)]
    start = 0
    for size in taper(main_units):
        cuts.append((start, size * unit))
        start += size * unit
    moves = []
    begin = 0
    for number, piece in enumerate(pieces):
        first, end = begin, begin + piece.shape[0]
        while first < end:
            rank = first // shard_rows
            stop = min(end, (rank + 1) * shard_rows)
            moves.append((number, first - begin, rank, first - rank * shard_rows, stop - first))
            first = stop
        begin = end
    slots = len(cuts) * (3 + (chips - 1) + 2 * (places - 1))
    vmem = pl.BlockSpec(memory_space=pltpu.VMEM)
    anywhere = pl.BlockSpec(memory_space=pl.ANY)
    bf16 = jnp.bfloat16
    out = pl.pallas_call(
        functools.partial(reduce_kernel, n_group, n_dp, cuts, moves),
        out_shape=jax.ShapeDtypeStruct((total_rows, LANES), bf16),
        in_specs=[anywhere] * (len(pieces) + 1),
        out_specs=vmem,
        scratch_shapes=[
            pltpu.VMEM((chips, 2, total_rows, LANES), bf16),
            pltpu.VMEM((chips, total_rows, LANES), bf16),
            pltpu.VMEM((chips - 1, total_rows, LANES), bf16),
            pltpu.VMEM((total_rows, LANES), bf16),
            pltpu.VMEM((total_rows // 2, LANES), bf16),
            pltpu.VMEM((total_rows // 2, LANES), bf16),
            pltpu.VMEM((places - 1, total_rows // n_dp, LANES), bf16),
            pltpu.SemaphoreType.DMA((slots,)),
            pltpu.SemaphoreType.DMA((slots,)),
            pltpu.SemaphoreType.DMA((len(moves) + 1,)),
        ],
        compiler_params=pltpu.CompilerParams(
            collective_id=1, has_side_effects=True, vmem_limit_bytes=22 * 1024 * 1024
        ),
    )(*pieces, gain_flat.reshape(chips, 2, tail_rows - spare, LANES))
    grad_shard = out[:shard_rows].reshape(-1).astype(jnp.float32)
    gain_shard = out[shard_rows : shard_rows + gain_rows].reshape(-1)[:gain_size]
    return grad_shard, gain_shard.reshape(-1, gain_cols).astype(jnp.float32)


def body(
    n_group,
    n_dp,
    hidden_in,
    out_grad,
    span_order,
    weights,
    first_moment,
    second_moment,
    gains,
    gain_first,
    gain_second,
):
    group_rank = lax.axis_index("group")
    seq_local = hidden_in.shape[0]
    slot_len = hidden_in.shape[1]
    width = hidden_in.shape[2]
    q_width = HEADS * HEAD_DIM
    kv_width = KV_HEADS * HEAD_DIM
    group_size = HEADS // KV_HEADS
    full_flat, full_gains = gather_weights(weights, gains, n_group, n_dp)
    w_query, w_key, w_value, w_out, w_gate, w_up, w_down = split_weights(full_flat)
    gain_attn = full_gains[0].astype(jnp.float32)
    gain_ffn = full_gains[1].astype(jnp.float32)
    offsets = jnp.arange(SPAN, dtype=jnp.int32)
    all_pos = (span_order[:, :, None] * SPAN + offsets[None, None, :]).reshape(seq_local, -1)
    local_pos = lax.dynamic_slice_in_dim(all_pos, group_rank * slot_len, slot_len, 1)
    cosine, sine_table = rope_tables(local_pos.reshape(-1))
    residual = hidden_in.reshape(-1, width).astype(jnp.float32)
    normed_one, factor_one = norm_forward(residual)
    attn_in = (normed_one * gain_attn).astype(jnp.bfloat16)
    query_proj = jnp.dot(attn_in, w_query, preferred_element_type=jnp.float32).reshape(
        -1, HEADS, HEAD_DIM
    )
    key_proj = jnp.dot(attn_in, w_key, preferred_element_type=jnp.float32).reshape(
        -1, KV_HEADS, HEAD_DIM
    )
    value_proj = jnp.dot(attn_in, w_value, preferred_element_type=jnp.float32)
    query_b = rotate(query_proj, cosine, sine_table).astype(jnp.bfloat16)
    key_b = rotate(key_proj, cosine, sine_table).astype(jnp.bfloat16).reshape(-1, kv_width)
    value_b = value_proj.astype(jnp.bfloat16)
    kv_local = jnp.concatenate([key_b, value_b], axis=-1).reshape(seq_local, slot_len, 2 * kv_width)
    kv_all = lax.all_gather(kv_local, "group", axis=1, tiled=True)
    query_seq = query_b.reshape(seq_local, slot_len, KV_HEADS, group_size, HEAD_DIM)
    attn_parts = []
    lse_parts = []
    for seq_index in range(seq_local):
        attn_one, lse_one = attend(
            query_seq[seq_index], kv_all[seq_index], local_pos[seq_index], all_pos[seq_index]
        )
        attn_parts.append(attn_one)
        lse_parts.append(lse_one)
    attn_b = jnp.concatenate(attn_parts, axis=0)
    middle = residual + jnp.dot(attn_b, w_out, preferred_element_type=jnp.float32)
    normed_two, factor_two = norm_forward(middle)
    ffn_in = (normed_two * gain_ffn).astype(jnp.bfloat16)
    gate_proj = jnp.dot(ffn_in, w_gate, preferred_element_type=jnp.float32)
    up_proj = jnp.dot(ffn_in, w_up, preferred_element_type=jnp.float32)
    sigmoid_gate = jax.nn.sigmoid(gate_proj)
    hidden = (gate_proj * sigmoid_gate * up_proj).astype(jnp.bfloat16)
    block_out = middle + jnp.dot(hidden, w_down, preferred_element_type=jnp.float32)
    grad_out = out_grad.reshape(-1, width)
    gw_down = outer_sum(hidden, grad_out)
    grad_hidden = jnp.dot(grad_out, w_down.T, preferred_element_type=jnp.float32)
    grad_gate = (
        grad_hidden * up_proj * sigmoid_gate * (1.0 + gate_proj * (1.0 - sigmoid_gate))
    ).astype(jnp.bfloat16)
    grad_up = (grad_hidden * gate_proj * sigmoid_gate).astype(jnp.bfloat16)
    gw_gate = outer_sum(ffn_in, grad_gate)
    gw_up = outer_sum(ffn_in, grad_up)
    grad_ffn_in = jnp.dot(grad_gate, w_gate.T, preferred_element_type=jnp.float32) + jnp.dot(
        grad_up, w_up.T, preferred_element_type=jnp.float32
    )
    gg_ffn = jnp.sum(grad_ffn_in * normed_two, axis=0)
    grad_middle = grad_out.astype(jnp.float32) + norm_backward(
        grad_ffn_in * gain_ffn, normed_two, factor_two
    )
    grad_middle_b = grad_middle.astype(jnp.bfloat16)
    gw_out = outer_sum(attn_b, grad_middle_b)
    grad_attn = jnp.dot(grad_middle_b, w_out.T, preferred_element_type=jnp.float32).astype(
        jnp.bfloat16
    )
    kv_back = lax.all_gather(kv_local, "group", axis=1, tiled=True)
    attn_seq = attn_b.reshape(seq_local, slot_len, q_width)
    grad_attn_seq = grad_attn.reshape(seq_local, slot_len, q_width)
    query_grads = []
    kv_grads = []
    for seq_index in range(seq_local):
        grad_query_one, grad_kv_one = attend_back(
            query_seq[seq_index],
            kv_back[seq_index],
            local_pos[seq_index],
            all_pos[seq_index],
            lse_parts[seq_index],
            attn_seq[seq_index],
            grad_attn_seq[seq_index],
        )
        query_grads.append(grad_query_one)
        kv_grads.append(grad_kv_one)
    grad_query = jnp.concatenate(query_grads, axis=0).reshape(-1, HEADS, HEAD_DIM)
    grad_kv_all = jnp.stack(kv_grads)
    grad_kv = lax.psum_scatter(grad_kv_all, "group", scatter_dimension=1, tiled=True).reshape(
        -1, 2 * kv_width
    )
    grad_query_b = (
        rotate_back(grad_query, cosine, sine_table).reshape(-1, q_width).astype(jnp.bfloat16)
    )
    grad_key_b = (
        rotate_back(grad_kv[:, :kv_width].reshape(-1, KV_HEADS, HEAD_DIM), cosine, sine_table)
        .reshape(-1, kv_width)
        .astype(jnp.bfloat16)
    )
    grad_value_b = grad_kv[:, kv_width:].astype(jnp.bfloat16)
    gw_query = outer_sum(attn_in, grad_query_b)
    gw_key = outer_sum(attn_in, grad_key_b)
    gw_value = outer_sum(attn_in, grad_value_b)
    grad_attn_in = jnp.dot(grad_query_b, w_query.T, preferred_element_type=jnp.float32)
    grad_attn_in = grad_attn_in + jnp.dot(grad_key_b, w_key.T, preferred_element_type=jnp.float32)
    grad_attn_in = grad_attn_in + jnp.dot(
        grad_value_b, w_value.T, preferred_element_type=jnp.float32
    )
    gg_attn = jnp.sum(grad_attn_in * normed_one, axis=0)
    in_grad = grad_middle + norm_backward(grad_attn_in * gain_attn, normed_one, factor_one)
    gain_grad = jnp.stack([gg_attn, gg_ffn])
    grad_shard, gain_shard = reduce_grads(
        (gw_query, gw_key, gw_value, gw_out, gw_gate, gw_up, gw_down),
        gain_grad.astype(jnp.bfloat16),
        n_group,
        n_dp,
    )
    new_weights, new_first, new_second = adamw_step(
        weights, first_moment, second_moment, grad_shard, DECAY_RATE, LEARN_RATE
    )
    new_gains, new_gain_first, new_gain_second = adamw_step(
        gains, gain_first, gain_second, gain_shard, 0.0, GAIN_RATE
    )
    return (
        block_out.reshape(seq_local, slot_len, width),
        in_grad.reshape(seq_local, slot_len, width),
        grad_shard,
        gain_shard,
        new_weights,
        new_first,
        new_second,
        new_gains,
        new_gain_first,
        new_gain_second,
    )


def solution(mesh):
    in_specs = (
        P("dp", "group", None),
        P("dp", "group", None),
        P("dp", None),
        P("group"),
        P("group"),
        P("group"),
        P(None, "group"),
        P(None, "group"),
        P(None, "group"),
    )
    out_specs = (
        P("dp", "group", None),
        P("dp", "group", None),
        P("group"),
        P(None, "group"),
        P("group"),
        P("group"),
        P("group"),
        P(None, "group"),
        P(None, "group"),
        P(None, "group"),
    )
    return jax.shard_map(
        functools.partial(body, mesh.shape["group"], mesh.shape["dp"]),
        mesh=mesh, in_specs=in_specs, out_specs=out_specs, check_vma=False)
```

```python
import functools

import jax
import jax.numpy as jnp
from jax import lax
from jax.experimental import pallas as pl
from jax.experimental.pallas import tpu as pltpu
from jax.sharding import PartitionSpec as P

D = 576
HEADS = 9
KV_HEADS = 3
HEAD_DIM = 64
FF = 1536
SPAN = 32


EPS_NORM = 1e-05
ROPE_BASE = 100000.0
BETA_ONE = 0.9
BETA_TWO = 0.95
LEARN_RATE = 0.02
GAIN_RATE = 0.25
DECAY_RATE = 0.1
EPS_ADAM = 1e-08
CORRECT_ONE = 1.0 - 0.9**5
CORRECT_TWO = 1.0 - 0.95**5
NEG_LARGE = -1e30
LANES = 128
TILE = 16


def split_weights(flat_vector, w_gate, w_up):
    q_width = HEADS * HEAD_DIM
    kv_width = KV_HEADS * HEAD_DIM
    layout = [(D, q_width), (D, kv_width), (D, kv_width), (q_width, D), (D, FF), (D, FF), (FF, D)]
    pieces = []
    offset = 0
    for rows_cols in layout:
        amount = rows_cols[0] * rows_cols[1]
        piece = lax.slice_in_dim(
            flat_vector, offset // LANES, (offset + amount) // LANES, axis=0
        )
        piece = lax.optimization_barrier(piece)
        pieces.append(piece.reshape(rows_cols))
        offset = offset + amount
    pieces[4], pieces[5] = w_gate, w_up
    return pieces


def rope_tables(positions):
    freq_index = jnp.arange(HEAD_DIM // 2, dtype=jnp.float32)
    inverse = ROPE_BASE ** (-2.0 * freq_index / HEAD_DIM)
    angles = positions.astype(jnp.float32)[:, None] * inverse[None, :]
    return (jnp.cos(angles), jnp.sin(angles))


def rotate(vectors, cosine, sine_table):
    half_dim = HEAD_DIM // 2
    first_half = vectors[..., :half_dim]
    second_half = vectors[..., half_dim:]
    cos_b = cosine[:, None, :]
    sin_b = sine_table[:, None, :]
    return jnp.concatenate(
        [first_half * cos_b - second_half * sin_b, second_half * cos_b + first_half * sin_b],
        axis=-1,
    )


def rotate_back(vectors, cosine, sine_table):
    half_dim = HEAD_DIM // 2
    first_half = vectors[..., :half_dim]
    second_half = vectors[..., half_dim:]
    cos_b = cosine[:, None, :]
    sin_b = sine_table[:, None, :]
    return jnp.concatenate(
        [first_half * cos_b + second_half * sin_b, second_half * cos_b - first_half * sin_b],
        axis=-1,
    )


def norm_forward(vectors):
    factor = lax.rsqrt(jnp.mean(vectors * vectors, axis=-1, keepdims=True) + EPS_NORM)
    return (vectors * factor, factor)


def norm_backward(grad_normed, normed, factor):
    return factor * (grad_normed - normed * jnp.mean(grad_normed * normed, axis=-1, keepdims=True))


def outer_sum(left_rows, right_rows):
    return lax.dot_general(
        left_rows, right_rows, (((0,), (0,)), ((), ())), preferred_element_type=jnp.float32
    )


def adamw_step(param_now, moment_one, moment_two, grad_now, decay_weight, step_rate):
    first_new = BETA_ONE * moment_one + (1.0 - BETA_ONE) * grad_now
    second_new = BETA_TWO * moment_two + (1.0 - BETA_TWO) * grad_now * grad_now
    update = first_new / CORRECT_ONE / (jnp.sqrt(second_new / CORRECT_TWO) + EPS_ADAM)
    return (param_now - step_rate * (update + decay_weight * param_now), first_new, second_new)


def split_pair(kv_seq):
    kv_width = KV_HEADS * HEAD_DIM
    key_blk = kv_seq[:, :kv_width].reshape(-1, KV_HEADS, HEAD_DIM)
    value_blk = kv_seq[:, kv_width:].reshape(-1, KV_HEADS, HEAD_DIM)
    return (key_blk, value_blk)


def masked_scores(query_blk, key_blk, query_pos, key_pos):
    scores = jnp.einsum(
        "qkgd,skd->kgqs", query_blk, key_blk, preferred_element_type=jnp.float32
    ) * HEAD_DIM ** (-0.5)
    allowed = key_pos[None, :] <= query_pos[:, None]
    return jnp.where(allowed[None, None], scores, NEG_LARGE)


def attend(query_blk, kv_seq, query_pos, key_pos):
    key_blk, value_blk = split_pair(kv_seq)
    scores = masked_scores(query_blk, key_blk, query_pos, key_pos)
    row_max = jnp.max(scores, axis=-1)
    log_total = row_max + jnp.log(jnp.sum(jnp.exp(scores - row_max[..., None]), axis=-1))
    probs_b = jnp.exp(scores - log_total[..., None]).astype(jnp.bfloat16)
    attn_vals = jnp.einsum("kgqs,skd->qkgd", probs_b, value_blk, preferred_element_type=jnp.float32)
    return (attn_vals.reshape(attn_vals.shape[0], -1).astype(jnp.bfloat16), log_total)


def attend_back(query_blk, kv_seq, query_pos, key_pos, log_total, attn_rows, grad_rows):
    group_size = HEADS // KV_HEADS
    key_blk, value_blk = split_pair(kv_seq)
    scores = masked_scores(query_blk, key_blk, query_pos, key_pos)
    probs = jnp.exp(scores - log_total[..., None])
    probs_b = probs.astype(jnp.bfloat16)
    grad_heads = grad_rows.reshape(-1, KV_HEADS, group_size, HEAD_DIM)
    attn_heads = attn_rows.reshape(-1, KV_HEADS, group_size, HEAD_DIM)
    delta_rows = jnp.einsum(
        "qkgd,qkgd->kgq", grad_heads, attn_heads, preferred_element_type=jnp.float32
    )
    grad_probs = jnp.einsum(
        "qkgd,skd->kgqs", grad_heads, value_blk, preferred_element_type=jnp.float32
    )
    grad_scores = (probs * (grad_probs - delta_rows[..., None]) * HEAD_DIM ** (-0.5)).astype(
        jnp.bfloat16
    )
    grad_query = jnp.einsum(
        "kgqs,skd->qkgd", grad_scores, key_blk, preferred_element_type=jnp.float32
    )
    grad_key = jnp.einsum(
        "kgqs,qkgd->skd", grad_scores, query_blk, preferred_element_type=jnp.float32
    )
    grad_value = jnp.einsum(
        "kgqs,qkgd->skd", probs_b, grad_heads, preferred_element_type=jnp.float32
    )
    key_rows = grad_key.shape[0]
    stacked = jnp.concatenate(
        [grad_key.reshape(key_rows, -1), grad_value.reshape(key_rows, -1)], axis=-1
    )
    return (grad_query, stacked)


def block_of(rows):
    for block in (144, 128, 96, 64, 48, 32):
        if rows % block == 0:
            return block
    return TILE


def over_rows(rows, step):
    block = block_of(rows)
    if rows == block:
        step(0, block)
        return

    def one(i, carry):
        step(pl.multiple_of(i * block, TILE), block)
        return carry

    lax.fori_loop(0, rows // block, one, 0)


def rows_at(start, size):
    return pl.ds(start if isinstance(start, int) else pl.multiple_of(start, TILE), size)


class Copies:
    def __init__(self, send_sem, recv_sem):
        self.send_sem, self.recv_sem, self.made = send_sem, recv_sem, []

    def start(self, src, dst, slot, where):
        copy = pltpu.make_async_remote_copy(
            src_ref=src,
            dst_ref=dst,
            send_sem=self.send_sem.at[slot],
            recv_sem=self.recv_sem.at[slot],
            device_id=where,
            device_id_type=pl.DeviceIdType.MESH,
        )
        copy.start()
        self.made.append(copy)

    def arrived(self, dst, slot, where):
        pltpu.make_async_remote_copy(
            src_ref=dst,
            dst_ref=dst,
            send_sem=self.send_sem.at[slot],
            recv_sem=self.recv_sem.at[slot],
            device_id=where,
            device_id_type=pl.DeviceIdType.MESH,
        ).wait_recv()

    def finish(self):
        for copy in self.made:
            copy.wait_send()


def greet(targets):
    barrier = pltpu.get_barrier_semaphore()
    for where in targets:
        pl.semaphore_signal(barrier, inc=1, device_id=where, device_id_type=pl.DeviceIdType.MESH)
    pl.semaphore_wait(barrier, len(targets))


def gather_kernel(
    n_group, n_dp, cuts, w_ref, g_ref, out_ref, gout_ref, gate_ref, up_ref,
    send_sem, recv_sem, local_sem,
):
    me, dp = lax.axis_index("group"), lax.axis_index("dp")
    core, chip, chips = me % 2, me // 2, n_group // 2
    sib = me + 1 - 2 * core
    half = dp % 2
    pair = dp + 1 - 2 * half
    half_rows = w_ref.shape[0] // 2
    at = lambda rank, d: {"group": rank, "dp": d}
    others = [(me + j) % n_group for j in range(1, n_group)]
    greet([at(rank, dp) for rank in others] + [at(me, pair)])
    copies = Copies(send_sem, recv_sem)
    n_cut = len(cuts)
    far = chips - 1
    base_far = 0
    base_pair = base_far + far * n_cut
    base_near = base_pair + far * n_cut
    base_near_pair = base_near + far * n_cut
    base_own = base_near_pair + far * n_cut
    base_gain = base_own + n_cut + 1
    gout_ref[pl.ds(me, 1)] = g_ref[...][None]

    blocks = FF // LANES
    kind = me // (n_group // 4)
    by_column = jnp.logical_or(kind == 1, kind == 2)

    def cast(start, rows):
        @pl.when(by_column)
        def _():
            column = start // rows

            def step(i, block):
                out_ref[me, rows_at(start + i, block), :] = w_ref[
                    pl.ds(i * blocks + column, block, stride=blocks), :
                ].astype(jnp.bfloat16)

            over_rows(rows, step)

        @pl.when(jnp.logical_not(by_column))
        def _():
            cast_rows(start, rows)

    def cast_rows(start, rows):
        def step(i, block):
            out_ref[me, rows_at(start + i, block), :] = w_ref[
                rows_at(start + i, block), :
            ].astype(jnp.bfloat16)

        over_rows(rows, step)

    starts = []
    start = 0
    for rows in cuts:
        starts.append(start)
        start += rows
    mine = half * half_rows
    theirs = (1 - half) * half_rows
    for c in range(n_cut):
        cast(mine + starts[c], cuts[c])
        piece = out_ref.at[me, rows_at(mine + starts[c], cuts[c]), :]
        for j in range(1, chips):
            to = ((chip + j) % chips) * 2 + core
            copies.start(piece, piece, base_far + (j - 1) * n_cut + c, at(to, dp))
        copies.start(piece, piece, base_own + c, at(sib, dp))
    for j in range(1, n_group):
        line = gout_ref.at[me]
        copies.start(line, line, base_gain + j - 1, at((me + j) % n_group, dp))
    for c in range(n_cut):
        cast(theirs + starts[c], cuts[c])
    rest = out_ref.at[me, rows_at(theirs, half_rows), :]
    copies.start(rest, rest, base_own + n_cut, at(sib, dp))
    for c in range(n_cut + 1):
        for j in range(1, chips):
            source = ((chip + chips - j) % chips) * 2 + core
            if c < n_cut:
                piece = out_ref.at[source, rows_at(mine + starts[c], cuts[c]), :]
                slot = (j - 1) * n_cut + c
                copies.arrived(piece, base_far + slot, at(source, dp))
                copies.start(piece, piece, base_pair + slot, at(me, pair))
                copies.start(piece, piece, base_near + slot, at(sib, dp))
            if c > 0:
                piece = out_ref.at[source, rows_at(theirs + starts[c - 1], cuts[c - 1]), :]
                slot = (j - 1) * n_cut + c - 1
                copies.arrived(piece, base_pair + slot, at(me, pair))
                copies.start(piece, piece, base_near_pair + slot, at(sib, dp))
    for c in range(n_cut):
        piece = out_ref.at[sib, rows_at(mine + starts[c], cuts[c]), :]
        copies.arrived(piece, base_own + c, at(sib, dp))
    rest = out_ref.at[sib, rows_at(theirs, half_rows), :]
    copies.arrived(rest, base_own + n_cut, at(sib, dp))
    for j in range(1, chips):
        source = ((chip + chips - j) % chips) * 2 + (1 - core)
        for c in range(n_cut):
            slot = (j - 1) * n_cut + c
            piece = out_ref.at[source, rows_at(mine + starts[c], cuts[c]), :]
            copies.arrived(piece, base_near + slot, at(sib, dp))
            piece = out_ref.at[source, rows_at(theirs + starts[c], cuts[c]), :]
            copies.arrived(piece, base_near_pair + slot, at(sib, dp))
    for j in range(1, n_group):
        source = (me + n_group - j) % n_group
        copies.arrived(gout_ref.at[source], base_gain + j - 1, at(source, dp))
    parts = n_group // 4
    depth = w_ref.shape[0] // blocks
    local = []
    for number, matrix in enumerate((gate_ref, up_ref)):
        for part in range(parts):
            for column in range(blocks):
                local.append(
                    pltpu.make_async_copy(
                        out_ref.at[(number + 1) * parts + part, pl.ds(column * depth, depth), :],
                        matrix.at[pl.ds(part * depth, depth), pl.ds(column * LANES, LANES)],
                        local_sem.at[len(local)],
                    )
                )
    for copy in local:
        copy.start()
    for copy in local:
        copy.wait()
    copies.finish()


def gather_weights(weights, gains, n_group, n_dp):
    rows = weights.shape[0] // LANES
    cuts = [rows * LANES // FF] * (FF // LANES // 2)
    gain_size = gains.shape[0] * gains.shape[1]
    gain_tile = (
        jnp.zeros((TILE * LANES,), jnp.bfloat16)
        .at[:gain_size]
        .set(gains.astype(jnp.bfloat16).reshape(-1))
        .reshape(TILE, LANES)
    )
    far = n_group // 2 - 1
    slots = 4 * far * len(cuts) + len(cuts) + 1 + n_group - 1
    vmem = pl.BlockSpec(memory_space=pltpu.VMEM)
    full, full_gains, w_gate, w_up = pl.pallas_call(
        functools.partial(gather_kernel, n_group, n_dp, cuts),
        out_shape=(
            jax.ShapeDtypeStruct((n_group, rows, LANES), jnp.bfloat16),
            jax.ShapeDtypeStruct((n_group, TILE, LANES), jnp.bfloat16),
            jax.ShapeDtypeStruct((D, FF), jnp.bfloat16),
            jax.ShapeDtypeStruct((D, FF), jnp.bfloat16),
        ),
        in_specs=[vmem, vmem],
        out_specs=(vmem, vmem, vmem, vmem),
        scratch_shapes=[
            pltpu.SemaphoreType.DMA((slots,)),
            pltpu.SemaphoreType.DMA((slots,)),
            pltpu.SemaphoreType.DMA((2 * (n_group // 4) * FF // LANES,)),
        ],
        compiler_params=pltpu.CompilerParams(
            collective_id=0, has_side_effects=True, vmem_limit_bytes=16 * 1024 * 1024
        ),
    )(weights.reshape(rows, LANES), gain_tile)
    full_gains = full_gains.reshape(n_group, -1)[:, :gain_size]
    full_gains = full_gains.reshape(n_group, gains.shape[0], gains.shape[1])
    full_gains = full_gains.transpose(1, 0, 2).reshape(gains.shape[0], -1)
    return full.reshape(-1, LANES), full_gains, w_gate, w_up


def reduce_kernel(n_group, n_dp, cuts, moves, *refs):
    pieces = refs[: 1 + max(move[0] for move in moves)]
    (gain_ref, result_ref, src, out_ref, buf1, buf2, sum2, buf3, sum3, buf4, send_sem, recv_sem, local_sem) = refs[
        len(pieces) :
    ]
    me, dp = lax.axis_index("group"), lax.axis_index("dp")
    core, chip, chips = me % 2, me // 2, n_group // 2
    sib = me + 1 - 2 * core
    half = dp % 2
    pair = dp + 1 - 2 * half
    place, places = dp // 2, n_dp // 2
    at = lambda rank, d: {"group": rank, "dp": d}
    far_to = [((chip + j) % chips) * 2 + core for j in range(1, chips)]
    line_to = [((place + j) % places) * 2 + half for j in range(1, places)]
    local = []
    for number, (piece, first, column, rank, row, rows) in enumerate(moves):
        local.append(
            pltpu.make_async_copy(
                pieces[piece].at[pl.ds(first, rows), pl.ds(column, LANES)],
                src.at[rank // 2, rank % 2, pl.ds(row, rows), :],
                local_sem.at[number],
            )
        )
    gain_rows = gain_ref.shape[2]
    local.append(
        pltpu.make_async_copy(
            gain_ref,
            src.at[:, :, pl.ds(src.shape[2] - gain_rows, gain_rows), :],
            local_sem.at[len(moves)],
        )
    )
    for copy in local:
        copy.start()
    greet(
        [at(sib, dp)] + [at(rank, dp) for rank in far_to]
        + [at(me, pair)] + [at(me, d) for d in line_to]
    )
    copies = Copies(send_sem, recv_sem)
    per = 3 + (chips - 1) + 2 * (places - 1)
    f32 = jnp.float32
    starts = [start for start, _ in cuts]
    cuts = [rows for _, rows in cuts]
    for copy in local:
        copy.wait()

    def send_core(c):
        rows = cuts[c]
        copies.start(
            src.at[:, 1 - core, pl.ds(starts[c], rows), :],
            buf1.at[:, pl.ds(starts[c], rows), :],
            c * per,
            at(sib, dp),
        )

    def after_core(c):
        rows, o = cuts[c], starts[c]
        copies.arrived(buf1.at[:, pl.ds(o, rows), :], c * per, at(sib, dp))
        for j in range(1, chips):
            k = (chip + j) % chips

            def step(i, block):
                here = rows_at(o + i, block)
                total = buf1[k, here, :].astype(f32) + src[k, core, here, :].astype(f32)
                buf1[k, here, :] = total.astype(jnp.bfloat16)

            over_rows(rows, step)
            copies.start(
                buf1.at[k, pl.ds(o, rows), :],
                buf2.at[j - 1, pl.ds(o, rows), :],
                c * per + j,
                at(far_to[j - 1], dp),
            )

    def after_far(c):
        rows, o = cuts[c], starts[c]
        for j in range(1, chips):
            copies.arrived(buf2.at[j - 1, pl.ds(o, rows), :], c * per + j, at(far_to[j - 1], dp))

        def step(i, block):
            here = rows_at(o + i, block)
            total = buf1[chip, here, :].astype(f32) + src[chip, core, here, :].astype(f32)
            for j in range(1, chips):
                total = total + buf2[j - 1, here, :].astype(f32)
            sum2[here, :] = total.astype(jnp.bfloat16)

        over_rows(rows, step)
        part = rows // 2
        copies.start(
            sum2.at[rows_at(o + (1 - half) * part, part), :],
            buf3.at[pl.ds(o // 2, part), :],
            c * per + chips,
            at(me, pair),
        )

    def after_pair(c):
        part, o = cuts[c] // 2, starts[c]
        copies.arrived(buf3.at[pl.ds(o // 2, part), :], c * per + chips, at(me, pair))

        def step(i, block):
            here = rows_at(o // 2 + i, block)
            total = sum2[rows_at(o + half * part + i, block), :].astype(f32)
            sum3[here, :] = (total + buf3[here, :].astype(f32)).astype(jnp.bfloat16)

        over_rows(part, step)
        piece = part // places
        for j in range(1, places):
            to = (place + j) % places
            copies.start(
                sum3.at[rows_at(o // 2 + to * piece, piece), :],
                buf4.at[j - 1, pl.ds(o // n_dp, piece), :],
                c * per + chips + j,
                at(me, line_to[j - 1]),
            )

    def after_line(c):
        part, o = cuts[c] // 2, starts[c]
        piece = part // places
        for j in range(1, places):
            copies.arrived(
                buf4.at[j - 1, pl.ds(o // n_dp, piece), :],
                c * per + chips + j,
                at(me, line_to[j - 1]),
            )
        first = o + half * part + place * piece

        def step(i, block):
            total = sum3[rows_at(o // 2 + place * piece + i, block), :].astype(f32)
            for j in range(1, places):
                total = total + buf4[j - 1, rows_at(o // n_dp + i, block), :].astype(f32)
            out_ref[rows_at(first + i, block), :] = total.astype(jnp.bfloat16)

        over_rows(piece, step)
        done = out_ref.at[rows_at(first, piece), :]
        for j in range(1, places):
            copies.start(done, done, c * per + chips + places - 1 + j, at(me, line_to[j - 1]))

    def after_back(c):
        part, o = cuts[c] // 2, starts[c]
        piece = part // places
        for j in range(1, places):
            origin = (place + places - j) % places
            copies.arrived(
                out_ref.at[rows_at(o + half * part + origin * piece, piece), :],
                c * per + chips + places - 1 + j,
                at(me, line_to[j - 1]),
            )
        done = out_ref.at[rows_at(o + half * part, part), :]
        copies.start(done, done, c * per + per - 1, at(me, pair))

    def last(c):
        part, o = cuts[c] // 2, starts[c]
        copies.arrived(
            out_ref.at[rows_at(o + (1 - half) * part, part), :], c * per + per - 1, at(me, pair)
        )

    n_cut = len(cuts)
    for c in range(n_cut):
        send_core(c)
    stages = [after_core, after_far, after_pair, after_line, after_back, last]
    lags = [0, 2, 3, 4, 5, 6]
    for t in range(n_cut + lags[-1]):
        for stage, lag in zip(stages, lags):
            if 0 <= t - lag < n_cut:
                stage(t - lag)
    blocks = FF // LANES
    kind = me // (n_group // 4)
    by_column = jnp.logical_or(kind == 1, kind == 2)
    shard_rows = src.shape[2] - gain_rows
    depth = shard_rows // blocks

    @pl.when(by_column)
    def _():
        for column in range(blocks):

            def step(i, block):
                result_ref[pl.ds(i * blocks + column, block, stride=blocks), :] = out_ref[
                    rows_at(column * depth + i, block), :
                ].astype(f32)

            over_rows(depth, step)

    @pl.when(jnp.logical_not(by_column))
    def _():
        def step(i, block):
            here = rows_at(i, block)
            result_ref[here, :] = out_ref[here, :].astype(f32)

        over_rows(shard_rows, step)

    result_ref[pl.ds(shard_rows, gain_rows), :] = out_ref[
        pl.ds(shard_rows, gain_rows), :
    ].astype(f32)
    copies.finish()


def taper(total_units):
    cap = -(-total_units // 6)
    sizes = []
    while total_units:
        size = min(total_units, max(3, min(cap, total_units // 3)))
        sizes.append(size)
        total_units -= size
    return sizes


def reduce_grads(weight_parts, gain_grad, n_group, n_dp):
    pieces = [part.astype(jnp.bfloat16) for part in weight_parts]
    pieces = [part if part.shape == (D, FF) else part.reshape(-1, LANES) for part in pieces]
    shard_rows = sum(piece.size for piece in pieces) // n_group // LANES
    unit = TILE * n_dp
    main_units = shard_rows // unit
    main_rows = main_units * unit
    spare = shard_rows - main_rows
    gain_cols = gain_grad.shape[1] // n_group
    gain_size = gain_grad.shape[0] * gain_cols
    gain_flat = gain_grad.reshape(-1, n_group, gain_cols).transpose(1, 0, 2).reshape(n_group, -1)
    gain_rows = -(-gain_size // LANES)
    tail_rows = -(-(spare + gain_rows) // unit) * unit
    gain_flat = jnp.pad(gain_flat, ((0, 0), (0, (tail_rows - spare) * LANES - gain_size)))
    total_rows = main_rows + tail_rows
    chips, places = n_group // 2, n_dp // 2
    cuts = [(main_rows, tail_rows)]
    start = 0
    for size in taper(main_units):
        cuts.append((start, size * unit))
        start += size * unit
    moves = []
    begin = 0
    for number, piece in enumerate(pieces):
        first, end = begin, begin + piece.size // LANES
        while first < end and piece.shape == (D, FF):
            depth = shard_rows * LANES // FF
            for column in range(FF // LANES):
                moves.append(
                    (
                        number,
                        (first - begin) * LANES // FF,
                        column * LANES,
                        first // shard_rows,
                        column * depth,
                        depth,
                    )
                )
            first += shard_rows
        while first < end:
            rank = first // shard_rows
            stop = min(end, (rank + 1) * shard_rows)
            moves.append(
                (number, first - begin, 0, rank, first - rank * shard_rows, stop - first)
            )
            first = stop
        begin = end
    slots = len(cuts) * (3 + (chips - 1) + 2 * (places - 1))
    vmem = pl.BlockSpec(memory_space=pltpu.VMEM)
    anywhere = pl.BlockSpec(memory_space=pltpu.HBM)
    bf16 = jnp.bfloat16
    out = pl.pallas_call(
        functools.partial(reduce_kernel, n_group, n_dp, cuts, moves),
        out_shape=jax.ShapeDtypeStruct((total_rows, LANES), jnp.float32),
        in_specs=[anywhere] * (len(pieces) + 1),
        out_specs=vmem,
        scratch_shapes=[
            pltpu.VMEM((chips, 2, total_rows, LANES), bf16),
            pltpu.VMEM((total_rows, LANES), bf16),
            pltpu.VMEM((chips, total_rows, LANES), bf16),
            pltpu.VMEM((chips - 1, total_rows, LANES), bf16),
            pltpu.VMEM((total_rows, LANES), bf16),
            pltpu.VMEM((total_rows // 2, LANES), bf16),
            pltpu.VMEM((total_rows // 2, LANES), bf16),
            pltpu.VMEM((places - 1, total_rows // n_dp, LANES), bf16),
            pltpu.SemaphoreType.DMA((slots,)),
            pltpu.SemaphoreType.DMA((slots,)),
            pltpu.SemaphoreType.DMA((len(moves) + 1,)),
        ],
        compiler_params=pltpu.CompilerParams(
            collective_id=1, has_side_effects=True, vmem_limit_bytes=26 * 1024 * 1024
        ),
    )(*pieces, gain_flat.reshape(chips, 2, tail_rows - spare, LANES))
    grad_shard = out[:shard_rows].reshape(-1)
    gain_shard = out[shard_rows : shard_rows + gain_rows].reshape(-1)[:gain_size]
    return grad_shard, gain_shard.reshape(-1, gain_cols)


def body(
    n_group,
    n_dp,
    hidden_in,
    out_grad,
    span_order,
    weights,
    first_moment,
    second_moment,
    gains,
    gain_first,
    gain_second,
):
    group_rank = lax.axis_index("group")
    seq_local = hidden_in.shape[0]
    slot_len = hidden_in.shape[1]
    width = hidden_in.shape[2]
    q_width = HEADS * HEAD_DIM
    kv_width = KV_HEADS * HEAD_DIM
    group_size = HEADS // KV_HEADS
    full_flat, full_gains, gathered_gate, gathered_up = gather_weights(weights, gains, n_group, n_dp)
    w_query, w_key, w_value, w_out, w_gate, w_up, w_down = split_weights(full_flat, gathered_gate, gathered_up)
    gain_attn = full_gains[0].astype(jnp.float32)
    gain_ffn = full_gains[1].astype(jnp.float32)
    offsets = jnp.arange(SPAN, dtype=jnp.int32)
    all_pos = (span_order[:, :, None] * SPAN + offsets[None, None, :]).reshape(seq_local, -1)
    local_pos = lax.dynamic_slice_in_dim(all_pos, group_rank * slot_len, slot_len, 1)
    cosine, sine_table = rope_tables(local_pos.reshape(-1))
    residual = hidden_in.reshape(-1, width).astype(jnp.float32)
    normed_one, factor_one = norm_forward(residual)
    attn_in = (normed_one * gain_attn).astype(jnp.bfloat16)
    query_proj = jnp.dot(attn_in, w_query, preferred_element_type=jnp.float32).reshape(
        -1, HEADS, HEAD_DIM
    )
    key_proj = jnp.dot(attn_in, w_key, preferred_element_type=jnp.float32).reshape(
        -1, KV_HEADS, HEAD_DIM
    )
    value_proj = jnp.dot(attn_in, w_value, preferred_element_type=jnp.float32)
    query_b = rotate(query_proj, cosine, sine_table).astype(jnp.bfloat16)
    key_b = rotate(key_proj, cosine, sine_table).astype(jnp.bfloat16).reshape(-1, kv_width)
    value_b = value_proj.astype(jnp.bfloat16)
    kv_local = jnp.concatenate([key_b, value_b], axis=-1).reshape(seq_local, slot_len, 2 * kv_width)
    kv_all = lax.all_gather(kv_local, "group", axis=1, tiled=True)
    query_seq = query_b.reshape(seq_local, slot_len, KV_HEADS, group_size, HEAD_DIM)
    attn_parts = []
    lse_parts = []
    for seq_index in range(seq_local):
        attn_one, lse_one = attend(
            query_seq[seq_index], kv_all[seq_index], local_pos[seq_index], all_pos[seq_index]
        )
        attn_parts.append(attn_one)
        lse_parts.append(lse_one)
    attn_b = jnp.concatenate(attn_parts, axis=0)
    middle = residual + jnp.dot(attn_b, w_out, preferred_element_type=jnp.float32)
    normed_two, factor_two = norm_forward(middle)
    ffn_in = (normed_two * gain_ffn).astype(jnp.bfloat16)
    gate_proj = jnp.dot(ffn_in, w_gate, preferred_element_type=jnp.float32)
    up_proj = jnp.dot(ffn_in, w_up, preferred_element_type=jnp.float32)
    sigmoid_gate = jax.nn.sigmoid(gate_proj)
    hidden = (gate_proj * sigmoid_gate * up_proj).astype(jnp.bfloat16)
    block_out = middle + jnp.dot(hidden, w_down, preferred_element_type=jnp.float32)
    grad_out = out_grad.reshape(-1, width)
    gw_down = outer_sum(hidden, grad_out)
    grad_hidden = jnp.dot(grad_out, w_down.T, preferred_element_type=jnp.float32)
    grad_gate = (
        grad_hidden * up_proj * sigmoid_gate * (1.0 + gate_proj * (1.0 - sigmoid_gate))
    ).astype(jnp.bfloat16)
    grad_up = (grad_hidden * gate_proj * sigmoid_gate).astype(jnp.bfloat16)
    gw_gate = outer_sum(ffn_in, grad_gate)
    gw_up = outer_sum(ffn_in, grad_up)
    grad_ffn_in = jnp.dot(grad_gate, w_gate.T, preferred_element_type=jnp.float32) + jnp.dot(
        grad_up, w_up.T, preferred_element_type=jnp.float32
    )
    gg_ffn = jnp.sum(grad_ffn_in * normed_two, axis=0)
    grad_middle = grad_out.astype(jnp.float32) + norm_backward(
        grad_ffn_in * gain_ffn, normed_two, factor_two
    )
    grad_middle_b = grad_middle.astype(jnp.bfloat16)
    gw_out = outer_sum(attn_b, grad_middle_b)
    grad_attn = jnp.dot(grad_middle_b, w_out.T, preferred_element_type=jnp.float32).astype(
        jnp.bfloat16
    )
    kv_back = lax.all_gather(kv_local, "group", axis=1, tiled=True)
    attn_seq = attn_b.reshape(seq_local, slot_len, q_width)
    grad_attn_seq = grad_attn.reshape(seq_local, slot_len, q_width)
    query_grads = []
    kv_grads = []
    for seq_index in range(seq_local):
        grad_query_one, grad_kv_one = attend_back(
            query_seq[seq_index],
            kv_back[seq_index],
            local_pos[seq_index],
            all_pos[seq_index],
            lse_parts[seq_index],
            attn_seq[seq_index],
            grad_attn_seq[seq_index],
        )
        query_grads.append(grad_query_one)
        kv_grads.append(grad_kv_one)
    grad_query = jnp.concatenate(query_grads, axis=0).reshape(-1, HEADS, HEAD_DIM)
    grad_kv_all = jnp.stack(kv_grads)
    grad_kv = lax.psum_scatter(grad_kv_all, "group", scatter_dimension=1, tiled=True).reshape(
        -1, 2 * kv_width
    )
    grad_query_b = (
        rotate_back(grad_query, cosine, sine_table).reshape(-1, q_width).astype(jnp.bfloat16)
    )
    grad_key_b = (
        rotate_back(grad_kv[:, :kv_width].reshape(-1, KV_HEADS, HEAD_DIM), cosine, sine_table)
        .reshape(-1, kv_width)
        .astype(jnp.bfloat16)
    )
    grad_value_b = grad_kv[:, kv_width:].astype(jnp.bfloat16)
    gw_query = outer_sum(attn_in, grad_query_b)
    gw_key = outer_sum(attn_in, grad_key_b)
    gw_value = outer_sum(attn_in, grad_value_b)
    grad_attn_in = jnp.dot(grad_query_b, w_query.T, preferred_element_type=jnp.float32)
    grad_attn_in = grad_attn_in + jnp.dot(grad_key_b, w_key.T, preferred_element_type=jnp.float32)
    grad_attn_in = grad_attn_in + jnp.dot(
        grad_value_b, w_value.T, preferred_element_type=jnp.float32
    )
    gg_attn = jnp.sum(grad_attn_in * normed_one, axis=0)
    in_grad = grad_middle + norm_backward(grad_attn_in * gain_attn, normed_one, factor_one)
    gain_grad = jnp.stack([gg_attn, gg_ffn])
    grad_shard, gain_shard = reduce_grads(
        (gw_query, gw_key, gw_value, gw_out, gw_gate, gw_up, gw_down),
        gain_grad.astype(jnp.bfloat16),
        n_group,
        n_dp,
    )
    new_weights, new_first, new_second = adamw_step(
        weights, first_moment, second_moment, grad_shard, DECAY_RATE, LEARN_RATE
    )
    new_gains, new_gain_first, new_gain_second = adamw_step(
        gains, gain_first, gain_second, gain_shard, 0.0, GAIN_RATE
    )
    return (
        block_out.reshape(seq_local, slot_len, width),
        in_grad.reshape(seq_local, slot_len, width),
        grad_shard,
        gain_shard,
        new_weights,
        new_first,
        new_second,
        new_gains,
        new_gain_first,
        new_gain_second,
    )


def solution(mesh):
    in_specs = (
        P("dp", "group", None),
        P("dp", "group", None),
        P("dp", None),
        P("group"),
        P("group"),
        P("group"),
        P(None, "group"),
        P(None, "group"),
        P(None, "group"),
    )
    out_specs = (
        P("dp", "group", None),
        P("dp", "group", None),
        P("group"),
        P(None, "group"),
        P("group"),
        P("group"),
        P("group"),
        P(None, "group"),
        P(None, "group"),
        P(None, "group"),
    )
    return jax.shard_map(
        functools.partial(body, mesh.shape["group"], mesh.shape["dp"]),
        mesh=mesh, in_specs=in_specs, out_specs=out_specs, check_vma=False)
```
